128 devices in a mesh: section: 8 (over z, x_lo), ctx: 16 (over y, x_hi, core).
Axes of the slice: x: 4 (x_hi: 2, x_lo: 2; x = x_hi * 2 + x_lo), y: 4, z: 4, core: 2. Of those that a mesh axis runs over, the one named last changes fastest.
Arguments:
- queries: bfloat16 [2, 8, 2048, 4096], P(None, 'section', 'ctx'), may hold values from -12 to 12
- keys: bfloat16 [2, 8, 2048, 512], P(None, 'section', 'ctx'), may hold values from -16 to 16
- values: bfloat16 [2, 8, 2048, 512], P(None, 'section', 'ctx'), may hold values from -4 to 4
- output_gradient: bfloat16 [2, 8, 2048, 4096], P(None, 'section', 'ctx'), may hold values from -12 to 12
- doc_tiles: int32 [2, 8, 4], P(None, 'section'), may hold values from 1 to 9, 16 in all within a row
- sink_logits: float32 [8, 32], replicated, may hold values from -1 to 3
Outputs:
- attention: bfloat16 [2, 8, 2048, 4096], P(None, 'section', 'ctx')
- query_grad: bfloat16 [2, 8, 2048, 4096], P(None, 'section', 'ctx')
- key_gradient: bfloat16 [2, 8, 2048, 512], P(None, 'section', 'ctx')
- value_gradient: bfloat16 [2, 8, 2048, 512], P(None, 'section', 'ctx')
- sink_grad: float32 [8, 32], P('section')
The draws below stay inside these ranges and needn't reach their ends.
Inputs may be any that keep to these rules, and one draw needn't show every extreme that they name: `doc_tiles`: the 4 lengths of each micro-batch sum to 16.
All inputs are finite; a program needn't handle non-finite values.
Results may differ from the reference program's by a relative error of at most 0.015.
Values may be sent and summed in bfloat16 or wider, within the bound.
No kernel may reach another device: no remote copies, remote signals or barrier semaphores. Data moves between devices by JAX's collectives and lax.ppermute only.
A program may use at most 128 MiB of HBM per device.

```python
import math
import jax
import jax.numpy as jnp
import numpy as np
from jax import lax

HEAD_WIDTH = 128
HQ = 32
KEY_HEADS = 4
QUERY_PER_KV = 8
TILE = 128
DOCS = 4
RELAY_COUNT = 2
SEQ_TOKENS = 2048
TILES = 16
N_SECTION = 8


def draw_keys(key, part):
    key = jax.random.fold_in(key, 11)
    noise_key, scale_key = jax.random.split(key)
    array_shape = (RELAY_COUNT, N_SECTION, SEQ_TOKENS, KEY_HEADS, HEAD_WIDTH)
    noise = jnp.clip(jax.random.normal(noise_key, array_shape, jnp.float32), -4.0, 4.0)
    row_scale = jnp.exp(jax.random.uniform(scale_key, array_shape[:4] + (1,), jnp.float32, math.log(0.4), math.log(4.0)))
    final_result = noise * row_scale
    return final_result.reshape(RELAY_COUNT, N_SECTION, SEQ_TOKENS, KEY_HEADS * HEAD_WIDTH).astype(jnp.bfloat16)


def draw_queries(key, part):
    key = jax.random.fold_in(key, 13)
    noise_key = jax.random.fold_in(key, 0)
    array_shape = (RELAY_COUNT, N_SECTION, SEQ_TOKENS, HQ, HEAD_WIDTH)
    final_result = jnp.clip(jax.random.normal(noise_key, array_shape, jnp.float32), -4.0, 4.0)
    return final_result.reshape(RELAY_COUNT, N_SECTION, SEQ_TOKENS, HQ * HEAD_WIDTH).astype(jnp.bfloat16)


def draw_output_gradient(key, part):
    key = jax.random.fold_in(key, 17)
    noise_key = jax.random.fold_in(key, 0)
    array_shape = (RELAY_COUNT, N_SECTION, SEQ_TOKENS, HQ * HEAD_WIDTH)
    rising = 1.0 + 2.0 * jnp.arange(SEQ_TOKENS, dtype=jnp.float32)[None, None, :, None] / SEQ_TOKENS
    final_result = jnp.clip(jax.random.normal(noise_key, array_shape, jnp.float32), -4.0, 4.0) * rising
    return final_result.astype(jnp.bfloat16)


def level_of(stream_key, shape, cuts, low, top_value):
    def one(dim, parts):
        draws = jax.random.uniform(jax.random.fold_in(jax.random.fold_in(stream_key, 6), dim), (parts,), jnp.float32, low / len(cuts), top_value / len(cuts))
        return jnp.repeat(jnp.exp(draws), shape[dim] // parts).reshape((-1,) + (1,) * (len(shape) - dim - 1))

    loudness = one(*cuts[0])
    for cut in cuts[1:]:
        loudness = loudness * one(*cut)
    return loudness


def split_up(amount, total, most, lean):
    weights = [(1 << 20) // math.isqrt(standing ** lean) + 1 for standing in range(2, amount + 1)]
    surplus, given = total - most - (amount - 1), [1] * (amount - 1)
    while surplus > 0:
        candidates = [i for i in range(amount - 1) if given[i] < most]
        pool, budget = sum([weights[i] for i in candidates]), surplus
        for i in candidates:
            extra = min(most - given[i], max(1, budget * weights[i] // pool), surplus)
            given[i] = given[i] + extra
            surplus = surplus - extra
    return np.array([most] + given)


def ragged_sizes(stream_key, amount, total, limit, slope):
    if amount == 2:
        one = jax.random.randint(stream_key, (), max(1, total - limit), min(limit, total - 1) + 1)
        return jnp.stack([one, total - one])
    sizes = jnp.asarray(split_up(amount, total, limit, slope), jnp.int32)
    couples = (amount - 1) // 2
    source_of, sink = sizes[1:1 + 2 * couples:2], sizes[2:2 + 2 * couples:2]
    slack = jnp.minimum(source_of - 1, limit - sink)
    passed = jax.random.randint(jax.random.fold_in(stream_key, 1), (couples,), 0, 1 << 20) % (slack + 1)
    sizes = sizes.at[1:1 + 2 * couples:2].set(source_of - passed).at[2:2 + 2 * couples:2].set(sink + passed)
    return sizes[jax.random.permutation(jax.random.fold_in(stream_key, 2), amount)]


def centred(rng, shape, spread, limit, cuts=(), kind=jnp.bfloat16):
    drawn = spread * jax.random.normal(rng, shape, jnp.float32)
    if cuts:
        drawn = drawn * level_of(rng, shape, cuts, -0.22, 0.18)
    return jnp.clip(drawn, -limit, limit).astype(kind)


def setup_inputs(seed: int = 0) -> dict:
    key_list = jax.random.split(jax.random.key(seed), 7)
    queries = draw_queries(jax.random.fold_in(key_list[6], 71), 0)
    keys = draw_keys(jax.random.fold_in(key_list[6], 71), 0)
    values = centred(key_list[2], (RELAY_COUNT, N_SECTION, SEQ_TOKENS, KEY_HEADS * HEAD_WIDTH), 1.0, 4.0, ((1, 8), (2, 16)))
    output_gradient = draw_output_gradient(jax.random.fold_in(key_list[6], 71), 0)
    doc_tiles = jax.vmap(lambda own: ragged_sizes(own, DOCS, TILES, TILES // 2 + 1, 2))(jax.random.split(key_list[4], RELAY_COUNT * N_SECTION)).reshape((RELAY_COUNT, N_SECTION, DOCS)).astype(jnp.int32)
    sink_logits = jnp.clip(jax.random.uniform(key_list[5], (N_SECTION, HQ), jnp.float32, -1.0, 3.0), -1.0, 3.0)
    return {"queries": queries, "keys": keys, "values": values, "output_gradient": output_gradient, "doc_tiles": doc_tiles, "sink_logits": sink_logits}


def one_head(packed, visible):
    query_head, grad_head, key_head, value_head, sink_head = packed
    scale = 1.0 / math.sqrt(HEAD_WIDTH)
    query_wide = query_head.astype(jnp.float32)
    grad_wide = grad_head.astype(jnp.float32)
    key_wide = key_head.astype(jnp.float32)
    value_wide = value_head.astype(jnp.float32)
    scores = jnp.einsum('tgd,ud->gtu', query_wide, key_wide) * scale
    masked = jnp.where(visible[None], scores, -jnp.inf)
    highest = jnp.maximum(lax.optimization_barrier(jnp.max(masked, axis=-1)), sink_head[:, None])
    log_total = highest + jnp.log(jnp.exp(sink_head[:, None] - highest) + lax.optimization_barrier(jnp.sum(jnp.exp(masked - highest[..., None]), axis=-1)))
    shares = jnp.exp(masked - log_total[..., None])
    shares_low = lax.optimization_barrier(shares.astype(jnp.bfloat16))
    heads = jnp.einsum('gtu,ud->gtd', shares_low.astype(jnp.float32), value_wide).astype(jnp.bfloat16)
    heads_kept = lax.optimization_barrier(heads)
    grad_by_head = jnp.transpose(grad_wide, (1, 0, 2))
    row_delta = lax.optimization_barrier(jnp.sum(grad_by_head * heads_kept.astype(jnp.float32), axis=-1))
    share_grads = jnp.einsum('tgd,ud->gtu', grad_wide, value_wide)
    score_grads = lax.optimization_barrier((shares * (share_grads - row_delta[..., None])).astype(jnp.bfloat16))
    score_wide = score_grads.astype(jnp.float32)
    query_grad = (jnp.einsum('gtu,ud->gtd', score_wide, key_wide) * scale).astype(jnp.bfloat16)
    key_gradient = (jnp.einsum('gtu,tgd->ud', score_wide, query_wide) * scale).astype(jnp.bfloat16)
    value_gradient = jnp.einsum('gtu,tgd->ud', shares_low.astype(jnp.float32), grad_wide).astype(jnp.bfloat16)
    sink_part = -lax.optimization_barrier(jnp.sum(jnp.exp(sink_head[:, None] - log_total) * row_delta, axis=-1))
    return (heads, query_grad, key_gradient, value_gradient, sink_part)

def micro_batch(packed):
    query_row_view, key_row_view, value_row_view, gradient_rows, lengths, sink_logit = packed
    positions = jnp.arange(SEQ_TOKENS, dtype=jnp.int32)
    ends = jnp.cumsum(lengths).astype(jnp.int32)
    document = lax.optimization_barrier(jnp.sum((positions[:, None] // TILE >= ends[None, :]).astype(jnp.int32), axis=1))
    visible = (document[:, None] == document[None, :]) & (positions[None, :] <= positions[:, None])
    query_head_view = jnp.transpose(query_row_view.reshape(SEQ_TOKENS, KEY_HEADS, QUERY_PER_KV, HEAD_WIDTH), (1, 0, 2, 3))
    gradient_heads = jnp.transpose(gradient_rows.reshape(SEQ_TOKENS, KEY_HEADS, QUERY_PER_KV, HEAD_WIDTH), (1, 0, 2, 3))
    key_head_view = jnp.transpose(key_row_view.reshape(SEQ_TOKENS, KEY_HEADS, HEAD_WIDTH), (1, 0, 2))
    value_head_view = jnp.transpose(value_row_view.reshape(SEQ_TOKENS, KEY_HEADS, HEAD_WIDTH), (1, 0, 2))
    sink_per_head = sink_logit.reshape(KEY_HEADS, QUERY_PER_KV)
    heads, query_grad, key_gradient, value_gradient, sink_part = lax.map(lambda packed_head: one_head(packed_head, visible), (query_head_view, gradient_heads, key_head_view, value_head_view, sink_per_head))
    attention = jnp.transpose(heads, (2, 0, 1, 3)).reshape(SEQ_TOKENS, HQ * HEAD_WIDTH)
    query_grad = jnp.transpose(query_grad, (2, 0, 1, 3)).reshape(SEQ_TOKENS, HQ * HEAD_WIDTH)
    key_gradient = jnp.transpose(key_gradient, (1, 0, 2)).reshape(SEQ_TOKENS, KEY_HEADS * HEAD_WIDTH)
    value_gradient = jnp.transpose(value_gradient, (1, 0, 2)).reshape(SEQ_TOKENS, KEY_HEADS * HEAD_WIDTH)
    return (attention, query_grad, key_gradient, value_gradient, sink_part.reshape(HQ))

def flatten_batch(array):
    return array.reshape((RELAY_COUNT * N_SECTION,) + array.shape[2:])

def reference(queries, keys, values, output_gradient, doc_tiles, sink_logits):
    layer_sinks = jnp.stack([sink_logits, sink_logits[::-1]])
    results = lax.map(micro_batch, (flatten_batch(queries), flatten_batch(keys), flatten_batch(values), flatten_batch(output_gradient), flatten_batch(doc_tiles), flatten_batch(layer_sinks)))
    attention, query_grad, key_gradient, value_gradient, sink_part = [item.reshape((RELAY_COUNT, N_SECTION) + item.shape[1:]) for item in results]
    sink_grad = sink_part[0] + sink_part[1][::-1]
    return (attention, query_grad, key_gradient, value_gradient, sink_grad)
```

```python
import functools
import math

import jax
import jax.numpy as jnp
from jax import lax
from jax.experimental import pallas as pl
from jax.experimental.pallas import tpu as pltpu
from jax.sharding import PartitionSpec as P

HEAD_WIDTH = 128
HQ = 32
KEY_HEADS = 4
QUERY_PER_KV = 8
TILE = 128
DOCS = 4
RELAY_COUNT = 2
LONGEST = 9
REACH = LONGEST // 2
ROWS = QUERY_PER_KV * TILE
KEY_COLS = KEY_HEADS * HEAD_WIDTH
QUERY_COLS = HQ * HEAD_WIDTH
SCALE = 1.0 / math.sqrt(HEAD_WIDTH)
LOG2E = 1.4426950408889634
HIDDEN = -1e30


def dot(left, right, left_dim, right_dim):
    return lax.dot_general(
        left,
        right,
        (((left_dim,), (right_dim,)), ((), ())),
        preferred_element_type=jnp.float32,
    )


def attend_kernel(meta, sink, q_ref, g_ref, *refs):
    mine = refs[: REACH + 1]
    mate = refs[REACH + 1 : 2 * REACH + 2]
    refs = refs[2 * REACH + 2 :]
    if len(refs) > 13:
        refs = refs[2:]
    o_ref, dq_ref, even, odd, sink_part = refs[:5]
    kv, grads, low_shares, low_scores, q_rows, g_rows, in_sem, out_sem = refs[5:]
    head = pl.program_id(0)
    count = meta[0]
    core = meta[1]

    def cols(j):
        return pl.ds(pl.multiple_of(j * HEAD_WIDTH, HEAD_WIDTH), HEAD_WIDTH)

    def fetch(j, slot, source):
        return pltpu.make_async_copy(
            source.at[:, :, cols(j)],
            kv.at[j, :, pl.ds(slot * TILE, TILE), :],
            in_sem.at[j, slot],
        )

    def give(j, slot):
        target = odd if slot % 2 else even
        return pltpu.make_async_copy(
            grads.at[j, :, pl.ds(slot * TILE, TILE), :],
            target.at[slot // 2, :, :, cols(j)],
            out_sem.at[j, slot],
        )

    @pl.when(head == 0)
    def _():
        for j in range(KEY_HEADS):
            for slot in range(LONGEST):

                @pl.when(count > slot)
                def _():
                    if slot % 2 == 0:
                        fetch(j, slot, mine[slot // 2]).start()
                    else:
                        near, far = mate[slot // 2], mate[slot // 2 + 1]
                        pl.when(core == 1)(lambda: fetch(j, slot, near).start())
                        pl.when(core == 0)(lambda: fetch(j, slot, far).start())

    for slot in range(LONGEST):
        pl.when(count > slot)(lambda: fetch(head, slot, mine[0]).wait())

    def case(tiles):
        width = tiles * TILE
        keys = kv[head, 0, :width, :]
        values = kv[head, 1, :width, :]
        heads = [slice(i * HEAD_WIDTH, (i + 1) * HEAD_WIDTH) for i in range(QUERY_PER_KV)]
        q = jnp.concatenate([q_ref[0, 0, :, part] for part in heads], axis=0)
        g = jnp.concatenate([g_ref[0, 0, :, part] for part in heads], axis=0)
        scores = dot(q, keys, 1, 1)
        row = lax.broadcasted_iota(jnp.int32, (TILE, TILE), 0)
        column = lax.broadcasted_iota(jnp.int32, (TILE, TILE), 1)
        seen = jnp.concatenate([column <= row] * QUERY_PER_KV, axis=0)
        own = jnp.where(seen, scores[:, :TILE], HIDDEN)
        scores = jnp.concatenate([own, scores[:, TILE:]], axis=1) if tiles > 1 else own
        logit = jnp.concatenate(
            [
                jnp.full((TILE, 1), sink[head * QUERY_PER_KV + i] * LOG2E, jnp.float32)
                for i in range(QUERY_PER_KV)
            ],
            axis=0,
        )
        top = jnp.maximum(jnp.max(scores, axis=1, keepdims=True) * (SCALE * LOG2E), logit)
        raised = jnp.exp2(scores * (SCALE * LOG2E) - top)
        low = raised.astype(jnp.bfloat16)
        low_shares[:, :width] = low
        sink_raised = jnp.exp2(logit - top)
        with_ones = jnp.concatenate([values, jnp.ones_like(values)], axis=1)
        sums = dot(low, with_ones, 1, 0)
        inverse = 1.0 / (sums[:, HEAD_WIDTH:] + sink_raised)
        out = (sums[:, :HEAD_WIDTH] * inverse).astype(jnp.bfloat16)
        g_wide = g.astype(jnp.float32)
        delta = jnp.sum(out.astype(jnp.float32) * g_wide, axis=1, keepdims=True)
        q_rows[...] = (q.astype(jnp.float32) * inverse).astype(jnp.bfloat16)
        g_rows[...] = (g_wide * inverse).astype(jnp.bfloat16)
        score_grads = (raised * (dot(g, values, 1, 1) - delta)).astype(jnp.bfloat16)
        low_scores[:, :width] = score_grads
        q_grad = (dot(score_grads, keys, 1, 0) * (inverse * SCALE)).astype(jnp.bfloat16)
        sink_rows = sink_raised * inverse * delta
        for i, part in enumerate(heads):
            rows = slice(i * TILE, (i + 1) * TILE)
            o_ref[0, 0, :, part] = out[rows]
            dq_ref[0, 0, :, part] = q_grad[rows]
            sink_part[0, i : i + 1, :] = -jnp.sum(sink_rows[rows], axis=0, keepdims=True)
        grads[head, 0, :width, :] = (
            dot(low_scores[:, :width], q_rows[...], 0, 0) * SCALE
        ).astype(jnp.bfloat16)
        grads[head, 1, :width, :] = dot(low_shares[:, :width], g_rows[...], 0, 0).astype(
            jnp.bfloat16
        )

    for tiles in range(1, LONGEST + 1):
        pl.when(count == tiles)(functools.partial(case, tiles))

    for slot in range(LONGEST):
        pl.when(count > slot)(lambda: give(head, slot).start())

    @pl.when(head == KEY_HEADS - 1)
    def _():
        for j in range(KEY_HEADS):
            for slot in range(LONGEST):
                pl.when(count > slot)(lambda: give(j, slot).wait())


def attend(relay, meta, sink, queries, output_gradient, mine, mate, filled):
    wide = pl.BlockSpec((1, 1, TILE, QUERY_PER_KV * HEAD_WIDTH), lambda j: (relay, 0, 0, j))
    smem = pl.BlockSpec(memory_space=pltpu.SMEM)
    whole = pl.BlockSpec(memory_space=pl.ANY)
    low = jnp.bfloat16
    first = 4 + len(mine) + len(mate)
    piece = (2, TILE, KEY_COLS)
    return pl.pallas_call(
        attend_kernel,
        grid=(KEY_HEADS,),
        in_specs=[smem, smem, wide, wide] + [whole] * (len(mine) + len(mate) + len(filled)),
        out_specs=[
            wide,
            wide,
            whole,
            whole,
            pl.BlockSpec((1, QUERY_PER_KV, HEAD_WIDTH), lambda j: (j, 0, 0)),
        ],
        out_shape=[
            jax.ShapeDtypeStruct((RELAY_COUNT, 1, TILE, QUERY_COLS), low),
            jax.ShapeDtypeStruct((RELAY_COUNT, 1, TILE, QUERY_COLS), low),
            jax.ShapeDtypeStruct((REACH + 1,) + piece, low),
            jax.ShapeDtypeStruct((REACH,) + piece, low),
            jax.ShapeDtypeStruct((KEY_HEADS, QUERY_PER_KV, HEAD_WIDTH), jnp.float32),
        ],
        scratch_shapes=[
            pltpu.VMEM((KEY_HEADS, 2, LONGEST * TILE, HEAD_WIDTH), low),
            pltpu.VMEM((KEY_HEADS, 2, LONGEST * TILE, HEAD_WIDTH), low),
            pltpu.VMEM((ROWS, LONGEST * TILE), low),
            pltpu.VMEM((ROWS, LONGEST * TILE), low),
            pltpu.VMEM((ROWS, HEAD_WIDTH), low),
            pltpu.VMEM((ROWS, HEAD_WIDTH), low),
            pltpu.SemaphoreType.DMA((KEY_HEADS, LONGEST)),
            pltpu.SemaphoreType.DMA((KEY_HEADS, LONGEST)),
        ],
        input_output_aliases={first + i: i for i in range(len(filled))},
        compiler_params=pltpu.CompilerParams(vmem_limit_bytes=48 * 1024 * 1024),
        cost_estimate=pl.CostEstimate(
            flops=10 * 6 * ROWS * KEY_COLS * TILE, bytes_accessed=9 << 20, transcendentals=1 << 20
        ),
        name=f"attend_{relay}",
    )(meta, sink, queries, output_gradient, *mine, *mate, *filled)


def shards(queries, keys, values, output_gradient, doc_tiles, sink_logits):
    ctx_count = lax.axis_size("ctx")
    ctx_pos = lax.axis_index("ctx")
    section_pos = lax.axis_index("section")
    section_count = lax.axis_size("section")
    core = lax.rem(ctx_pos, 2)

    def back(amount):
        return [(c, c - amount) for c in range(ctx_count) if 0 <= c - amount < ctx_count]

    def other(moving):
        return [(c, c ^ 1) for c in range(ctx_count) if moving(c)]

    def seen_by(position):
        ends = jnp.cumsum(doc_tiles[:, 0], axis=-1)
        start = jnp.max(jnp.where(ends <= position, ends, 0), axis=-1)
        return position - start + 1

    counts = seen_by(ctx_pos)
    mate_counts = seen_by(ctx_pos + 1 - 2 * core)

    pieces = [jnp.stack([keys[r, 0], values[r, 0]]) for r in range(RELAY_COUNT)]
    mines, mates = {}, {}
    for relay in (1, 0):
        mine = [pieces[relay]]
        for distance in range(1, REACH + 1):
            mine.append(lax.ppermute(pieces[relay], "ctx", back(-2 * distance)))
        mate = [
            lax.ppermute(
                piece,
                "ctx",
                other(
                    lambda c: (c % 2 == 1 or distance < REACH) and (c % 2 == 0 or distance > 0)
                ),
            )
            for distance, piece in enumerate(mine)
        ]
        mines[relay], mates[relay] = mine, mate

    filled = []
    outs, sinks = {}, {}
    for relay in (1, 0):
        layer = section_pos if relay == 0 else section_count - 1 - section_pos
        sink = lax.dynamic_index_in_dim(sink_logits, layer, 0, keepdims=False)
        meta = jnp.stack([counts[relay], core]).astype(jnp.int32)
        attention, query_grad, even, odd, sink_part = attend(
            relay, meta, sink, queries, output_gradient, mines[relay], mates[relay], filled
        )
        filled = [attention, query_grad]
        sinks[relay] = sink_part[:, :, 0].reshape(HQ)
        from_mate = lax.ppermute(odd, "ctx", other(lambda c: True))
        total = None
        for distance in range(REACH + 1):
            theirs = distance - core
            slot = 2 * theirs + 1
            term = jnp.where(
                counts[relay] > 2 * distance, even[distance].astype(jnp.float32), 0.0
            ) + jnp.where(
                (theirs >= 0) & (theirs < REACH) & (mate_counts[relay] > slot),
                lax.dynamic_index_in_dim(
                    from_mate, jnp.clip(theirs, 0, REACH - 1), 0, keepdims=False
                ).astype(jnp.float32),
                0.0,
            )
            if distance == 0:
                total = term
            else:
                sent = lax.ppermute(term.astype(jnp.bfloat16), "ctx", back(2 * distance))
                total = total + sent.astype(jnp.float32)
        outs[relay] = total.astype(jnp.bfloat16)

    mirrored = lax.ppermute(
        sinks[1], "section", [(s, section_count - 1 - s) for s in range(section_count)]
    )
    sink_grad = sinks[0] + mirrored
    step = 1
    while step < ctx_count:
        sink_grad = sink_grad + lax.ppermute(
            sink_grad, "ctx", [(c, c ^ step) for c in range(ctx_count)]
        )
        step *= 2
    attention, query_grad = filled
    key_gradient = jnp.stack([outs[r][0] for r in range(RELAY_COUNT)])[:, None]
    value_gradient = jnp.stack([outs[r][1] for r in range(RELAY_COUNT)])[:, None]
    return (attention, query_grad, key_gradient, value_gradient, sink_grad[None])


def solution(mesh):
    placed = (
        P(None, "section", "ctx", None),
        P(None, "section", "ctx", None),
        P(None, "section", "ctx", None),
        P(None, "section", "ctx", None),
        P(None, "section", None),
        P(),
    )
    return jax.shard_map(
        shards,
        mesh=mesh,
        in_specs=placed,
        out_specs=(
            P(None, "section", "ctx", None),
            P(None, "section", "ctx", None),
            P(None, "section", "ctx", None),
            P(None, "section", "ctx", None),
            P("section", None),
        ),
        check_vma=False,
    )
```

```python
import functools
import math

import jax
import jax.numpy as jnp
from jax import lax
from jax.experimental import pallas as pl
from jax.experimental.pallas import tpu as pltpu
from jax.sharding import PartitionSpec as P

HEAD_WIDTH = 128
HQ = 32
KEY_HEADS = 4
QUERY_PER_KV = 8
TILE = 128
DOCS = 4
RELAY_COUNT = 2
LONGEST = 9
REACH = LONGEST // 2
ROWS = QUERY_PER_KV * TILE
KEY_COLS = KEY_HEADS * HEAD_WIDTH
QUERY_COLS = HQ * HEAD_WIDTH
SCALE = 1.0 / math.sqrt(HEAD_WIDTH)
LOG2E = 1.4426950408889634
HIDDEN = -1e30
GROUP = 3
SLOTS = -(-LONGEST // GROUP) * GROUP
PART = 1024


def dot(left, right, left_dim, right_dim):
    return lax.dot_general(
        left,
        right,
        (((left_dim,), (right_dim,)), ((), ())),
        preferred_element_type=jnp.float32,
    )


def attend_kernel(meta, sink, q_ref, g_ref, *refs):
    mine = refs[: REACH + 1]
    mate = refs[REACH + 1 : 2 * REACH + 2]
    refs = refs[2 * REACH + 2 :]
    if len(refs) > 16:
        refs = refs[2:]
    o_ref, dq_ref, even, odd, sink_part = refs[:5]
    kv, grads, q_turned, g_turned, q_rows, g_rows, scores, shares, out_sum, dq_sum = refs[5:15]
    (sems,) = refs[15:]
    in_sem, out_sem = sems.at[0], sems.at[1]
    head = pl.program_id(0)
    count = meta[0]
    core = meta[1]
    pairs = lax.div(count + GROUP - 1, GROUP)
    PAIR = GROUP * TILE

    def cols(j):
        return pl.ds(pl.multiple_of(j * HEAD_WIDTH, HEAD_WIDTH), HEAD_WIDTH)

    def fetch(j, slot, source):
        return pltpu.make_async_copy(
            source.at[:, :, cols(j)],
            kv.at[j, :, pl.ds(slot * TILE, TILE), :],
            in_sem.at[j, slot],
        )

    def give(j, slot):
        target = odd if slot % 2 else even
        return pltpu.make_async_copy(
            grads.at[j, :, pl.ds(slot * TILE, TILE), :],
            target.at[slot // 2, :, :, cols(j)],
            out_sem.at[j, slot],
        )

    @pl.when(head == 0)
    def _():
        for j in range(KEY_HEADS):
            for slot in range(LONGEST):

                @pl.when(count > slot)
                def _():
                    if slot % 2 == 0:
                        fetch(j, slot, mine[slot // 2]).start()
                    else:
                        near, far = mate[slot // 2], mate[slot // 2 + 1]
                        pl.when(core == 1)(lambda: fetch(j, slot, near).start())
                        pl.when(core == 0)(lambda: fetch(j, slot, far).start())

        for slot in range(1, SLOTS):

            @pl.when((slot >= count) & (slot < pairs * GROUP))
            def _():
                for j in range(KEY_HEADS):
                    kv[j, :, slot * TILE : (slot + 1) * TILE, :] = jnp.zeros(
                        (2, TILE, HEAD_WIDTH), jnp.bfloat16
                    )

    heads = [slice(i * HEAD_WIDTH, (i + 1) * HEAD_WIDTH) for i in range(QUERY_PER_KV)]
    parts = [slice(i * PART, (i + 1) * PART) for i in range(ROWS // PART)]
    for part in heads:
        q, g = q_ref[0, 0, :, part], g_ref[0, 0, :, part]
        q_rows[part, :] = q
        g_rows[part, :] = g
        q_turned[:, part] = q.T
        g_turned[:, part] = g.T

    for slot in range(LONGEST):
        pl.when(count > slot)(lambda: fetch(head, slot, mine[0]).wait())

    def block(pair):
        return pl.ds(pl.multiple_of(pair * PAIR, PAIR), PAIR)

    def hide_spare(pair, score):
        rows = [score[:TILE]]
        for i in range(1, GROUP):
            bias = jnp.where(GROUP * pair + i < count, 0.0, HIDDEN).astype(jnp.float32)
            rows.append(score[i * TILE : (i + 1) * TILE] + bias)
        return jnp.concatenate(rows, axis=0)

    row = lax.broadcasted_iota(jnp.int32, (TILE, TILE), 0)
    column = lax.broadcasted_iota(jnp.int32, (TILE, TILE), 1)
    seen = jnp.concatenate([row <= column] * (PART // TILE), axis=1)
    tops = []
    for part in parts:
        score = hide_spare(0, dot(kv[head, 0, :PAIR, :], q_turned[:, part], 1, 0))
        score = jnp.concatenate([jnp.where(seen, score[:TILE], HIDDEN), score[TILE:]], axis=0)
        scores[:PAIR, part] = score
        tops.append(jnp.max(score.reshape(-1, 8, PART), axis=0))

    def score_step(pair, tops):
        keys = kv[head, 0, block(pair), :]
        new = []
        for part, top in zip(parts, tops):
            score = hide_spare(pair, dot(keys, q_turned[:, part], 1, 0))
            scores[block(pair), part] = score
            new.append(jnp.maximum(top, jnp.max(score.reshape(-1, 8, PART), axis=0)))
        return tuple(new)

    tops = lax.fori_loop(1, pairs, score_step, tuple(tops))
    logit = jnp.concatenate(
        [
            jnp.full((1, TILE), sink[head * QUERY_PER_KV + i] * LOG2E, jnp.float32)
            for i in range(QUERY_PER_KV)
        ],
        axis=1,
    )
    logits = [logit[:, part] for part in parts]
    tops = [
        jnp.maximum(jnp.max(top, axis=0, keepdims=True) * (SCALE * LOG2E), one)
        for top, one in zip(tops, logits)
    ]

    out_sum[...] = jnp.zeros_like(out_sum)
    dq_sum[...] = jnp.zeros_like(dq_sum)
    ones = jnp.ones((16, PAIR), jnp.bfloat16)

    def share_step(pair, carry):
        turned = jnp.concatenate([kv[head, 1, block(pair), :].T, ones], axis=0)
        for part, top in zip(parts, tops):
            low = jnp.exp2(scores[block(pair), part] * (SCALE * LOG2E) - top).astype(jnp.bfloat16)
            shares[block(pair), part] = low
            out_sum[:, part] += dot(turned, low, 1, 0)
        return carry

    lax.fori_loop(0, pairs, share_step, 0)
    inverses, deltas = [], []
    for i, part in enumerate(parts):
        sink_raised = jnp.exp2(logits[i] - tops[i])
        inverse = 1.0 / (out_sum[HEAD_WIDTH : HEAD_WIDTH + 1, part] + sink_raised)
        out = (out_sum[:HEAD_WIDTH, part] * inverse).astype(jnp.bfloat16)
        delta = jnp.sum(
            out.astype(jnp.float32) * g_turned[:, part].astype(jnp.float32), axis=0, keepdims=True
        )
        sink_rows = sink_raised * inverse * delta
        for k in range(PART // TILE):
            h = i * (PART // TILE) + k
            inner = slice(k * TILE, (k + 1) * TILE)
            o_ref[0, 0, :, heads[h]] = out[:, inner].T
            sink_part[0, h : h + 1, :] = jnp.broadcast_to(
                -jnp.sum(sink_rows[:, inner], axis=1, keepdims=True), (1, HEAD_WIDTH)
            )
        inverses.append(inverse)
        deltas.append(delta)

    def grad_step(pair, carry):
        keys = kv[head, 0, block(pair), :]
        values = kv[head, 1, block(pair), :]
        turned = keys.T
        key_grad = value_grad = None
        for i, part in enumerate(parts):
            share = shares[block(pair), part].astype(jnp.float32) * inverses[i]
            share_grad = dot(values, g_turned[:, part], 1, 0)
            score_grad = (share * (share_grad - deltas[i])).astype(jnp.bfloat16)
            dq_sum[:, part] += dot(turned, score_grad, 1, 0)
            one = dot(score_grad, q_rows[part, :], 1, 0)
            two = dot(share.astype(jnp.bfloat16), g_rows[part, :], 1, 0)
            key_grad = one if key_grad is None else key_grad + one
            value_grad = two if value_grad is None else value_grad + two
        grads[head, 0, block(pair), :] = (key_grad * SCALE).astype(jnp.bfloat16)
        grads[head, 1, block(pair), :] = value_grad.astype(jnp.bfloat16)
        return carry

    lax.fori_loop(0, pairs, grad_step, 0)
    for slot in range(LONGEST):
        pl.when(count > slot)(lambda: give(head, slot).start())
    for part in heads:
        dq_ref[0, 0, :, part] = (dq_sum[:, part] * SCALE).astype(jnp.bfloat16).T

    @pl.when(head == KEY_HEADS - 1)
    def _():
        for j in range(KEY_HEADS):
            for slot in range(LONGEST):
                pl.when(count > slot)(lambda: give(j, slot).wait())


def attend(relay, meta, sink, queries, output_gradient, mine, mate, filled):
    wide = pl.BlockSpec((1, 1, TILE, QUERY_PER_KV * HEAD_WIDTH), lambda j: (relay, 0, 0, j))
    smem = pl.BlockSpec(memory_space=pltpu.SMEM)
    whole = pl.BlockSpec(memory_space=pl.ANY)
    low = jnp.bfloat16
    first = 4 + len(mine) + len(mate)
    piece = (2, TILE, KEY_COLS)
    return pl.pallas_call(
        attend_kernel,
        grid=(KEY_HEADS,),
        in_specs=[smem, smem, wide, wide] + [whole] * (len(mine) + len(mate) + len(filled)),
        out_specs=[
            wide,
            wide,
            whole,
            whole,
            pl.BlockSpec((1, QUERY_PER_KV, HEAD_WIDTH), lambda j: (j, 0, 0)),
        ],
        out_shape=[
            jax.ShapeDtypeStruct((RELAY_COUNT, 1, TILE, QUERY_COLS), low),
            jax.ShapeDtypeStruct((RELAY_COUNT, 1, TILE, QUERY_COLS), low),
            jax.ShapeDtypeStruct((REACH + 1,) + piece, low),
            jax.ShapeDtypeStruct((REACH,) + piece, low),
            jax.ShapeDtypeStruct((KEY_HEADS, QUERY_PER_KV, HEAD_WIDTH), jnp.float32),
        ],
        scratch_shapes=[
            pltpu.VMEM((KEY_HEADS, 2, SLOTS * TILE, HEAD_WIDTH), low),
            pltpu.VMEM((KEY_HEADS, 2, SLOTS * TILE, HEAD_WIDTH), low),
            pltpu.VMEM((HEAD_WIDTH, ROWS), low),
            pltpu.VMEM((HEAD_WIDTH, ROWS), low),
            pltpu.VMEM((ROWS, HEAD_WIDTH), low),
            pltpu.VMEM((ROWS, HEAD_WIDTH), low),
            pltpu.VMEM((SLOTS * TILE, ROWS), jnp.float32),
            pltpu.VMEM((SLOTS * TILE, ROWS), low),
            pltpu.VMEM((HEAD_WIDTH + 16, ROWS), jnp.float32),
            pltpu.VMEM((HEAD_WIDTH, ROWS), jnp.float32),
            pltpu.SemaphoreType.DMA((2, KEY_HEADS, LONGEST)),
        ],
        input_output_aliases={first + i: i for i in range(len(filled))},
        compiler_params=pltpu.CompilerParams(vmem_limit_bytes=36 * 1024 * 1024),
        cost_estimate=pl.CostEstimate(
            flops=12 * LONGEST * HQ * TILE * TILE * HEAD_WIDTH * 4,
            bytes_accessed=9 << 20,
            transcendentals=LONGEST * HQ * TILE * TILE,
        ),
        name=f"attend_{relay}",
    )(meta, sink, queries, output_gradient, *mine, *mate, *filled)


def shards(queries, keys, values, output_gradient, doc_tiles, sink_logits):
    ctx_count = lax.axis_size("ctx")
    ctx_pos = lax.axis_index("ctx")
    section_pos = lax.axis_index("section")
    section_count = lax.axis_size("section")
    core = lax.rem(ctx_pos, 2)

    def back(amount):
        return [(c, c - amount) for c in range(ctx_count) if 0 <= c - amount < ctx_count]

    def other(moving):
        return [(c, c ^ 1) for c in range(ctx_count) if moving(c)]

    def seen_by(position):
        counts = []
        for relay in range(RELAY_COUNT):
            end = start = jnp.zeros((), jnp.int32)
            for document in range(DOCS):
                end = end + doc_tiles[relay, 0, document]
                start = jnp.where(end <= position, end, start)
            counts.append(position - start + 1)
        return counts

    counts = seen_by(ctx_pos)
    mate_counts = seen_by(ctx_pos + 1 - 2 * core)

    def sink_of(relay):
        layer = section_pos if relay == 0 else section_count - 1 - section_pos
        return lax.dynamic_index_in_dim(sink_logits, layer, 0, keepdims=False)

    def meta_of(relay):
        return jnp.stack([counts[relay], core]).astype(jnp.int32)

    def fetched(piece):
        return [piece] + [
            lax.ppermute(piece, "ctx", back(-2 * distance)) for distance in range(1, REACH + 1)
        ]

    def swapped(pieces):
        return [lax.ppermute(piece, "ctx", other(lambda c: True)) for piece in pieces]

    def chip_terms(relay, even, odd):
        from_mate = lax.ppermute(odd, "ctx", other(lambda c: True))
        terms = []
        for distance in range(REACH + 1):
            theirs = distance - core
            known = (theirs >= 0) & (theirs < REACH) & (mate_counts[relay] > 2 * theirs + 1)
            own = even[distance].astype(jnp.float32)
            added = lax.dynamic_index_in_dim(
                from_mate, jnp.clip(theirs, 0, REACH - 1), 0, keepdims=False
            ).astype(jnp.float32)
            term = jnp.where(counts[relay] > 2 * distance, own, 0.0) + jnp.where(known, added, 0.0)
            terms.append(term if distance == 0 else term.astype(jnp.bfloat16))
        return terms

    def returned(terms):
        return [
            lax.ppermute(terms[distance], "ctx", back(2 * distance))
            for distance in range(1, REACH + 1)
        ]

    def summed(own, others):
        for other_term in others:
            own = own + other_term.astype(jnp.float32)
        return own.astype(jnp.bfloat16)

    first, second = 1, 0
    pieces = [jnp.stack([keys[r, 0], values[r, 0]]) for r in range(RELAY_COUNT)]
    mine_first = fetched(pieces[first])
    own_swapped = swapped([pieces[second]])
    mine_second = fetched(pieces[second])
    attention, query_grad, even, odd, sink_part = attend(
        first,
        meta_of(first),
        sink_of(first),
        queries,
        output_gradient,
        mine_first,
        swapped(mine_first),
        [],
    )
    mine_second, sink_part, odd = lax.optimization_barrier((mine_second, sink_part, odd))
    terms_first = chip_terms(first, even, odd)
    mate_second = own_swapped + swapped(mine_second[1:])
    mirrored = lax.ppermute(
        sink_part[:, :, 0].reshape(HQ),
        "section",
        [(s, section_count - 1 - s) for s in range(section_count)],
    )
    meta, mate_second, mirrored, terms_first = lax.optimization_barrier(
        (meta_of(second), mate_second, mirrored, terms_first)
    )
    sent_first = returned(terms_first)
    attention, query_grad, even, odd, sink_part = attend(
        second,
        meta,
        sink_of(second),
        queries,
        output_gradient,
        mine_second,
        mate_second,
        [attention, query_grad],
    )
    sent_first, sink_part, odd = lax.optimization_barrier((sent_first, sink_part, odd))
    terms_second = chip_terms(second, even, odd)
    sink_grad = sink_part[:, :, 0].reshape(HQ) + mirrored
    sink_grad, terms_second = lax.optimization_barrier((sink_grad, terms_second))
    sent_second = returned(terms_second)
    step = 1
    while step < ctx_count:
        sink_grad = sink_grad + lax.ppermute(
            sink_grad, "ctx", [(c, c ^ step) for c in range(ctx_count)]
        )
        step *= 2
    first_sum = summed(terms_first[0], sent_first)
    sent_second, sink_grad, first_sum = lax.optimization_barrier(
        (sent_second, sink_grad, first_sum)
    )
    second_sum = summed(terms_second[0], sent_second)
    key_gradient = jnp.stack([second_sum[0], first_sum[0]])[:, None]
    value_gradient = jnp.stack([second_sum[1], first_sum[1]])[:, None]
    return (attention, query_grad, key_gradient, value_gradient, sink_grad[None])


def solution(mesh):
    placed = (
        P(None, "section", "ctx", None),
        P(None, "section", "ctx", None),
        P(None, "section", "ctx", None),
        P(None, "section", "ctx", None),
        P(None, "section", None),
        P(),
    )
    return jax.shard_map(
        shards,
        mesh=mesh,
        in_specs=placed,
        out_specs=(
            P(None, "section", "ctx", None),
            P(None, "section", "ctx", None),
            P(None, "section", "ctx", None),
            P(None, "section", "ctx", None),
            P("section", None),
        ),
        check_vma=False,
    )
```

```python
import functools
import math

import jax
import jax.numpy as jnp
from jax import lax
from jax.experimental import pallas as pl
from jax.experimental.pallas import tpu as pltpu
from jax.sharding import PartitionSpec as P

HEAD_WIDTH = 128
HQ = 32
KEY_HEADS = 4
QUERY_PER_KV = 8
TILE = 128
DOCS = 4
RELAY_COUNT = 2
LONGEST = 9
REACH = LONGEST // 2
ROWS = QUERY_PER_KV * TILE
SCALE = 1.0 / math.sqrt(HEAD_WIDTH)
LOG2E = 1.4426950408889634
HIDDEN = -1e30
VMEM_BYTES = 26 * 1024 * 1024
GROUP = 3
SLOTS = 2 * (REACH + 1)
HEADS = KEY_HEADS // 2
STEPS = 2 * HEADS
KEY_PART = HEADS * HEAD_WIDTH
WIDE = QUERY_PER_KV * HEAD_WIDTH
QUERY_PART = HEADS * WIDE


def dot(left, right, left_dim, right_dim):
    return lax.dot_general(
        left,
        right,
        (((left_dim,), (right_dim,)), ((), ())),
        preferred_element_type=jnp.float32,
    )


def attend_kernel(relay, refilled, meta, sink, q_own, g_own, q_got, g_got, *refs):
    pieces = refs[: REACH + 1]
    refs = refs[REACH + 1 + refilled :]
    o_ref, dq_ref, out_send = refs[:3]
    terms = refs[3 : REACH + 4]
    sink_part = refs[REACH + 4]
    q_in, g_in, o_out, dq_out, kv, grads, grads_low = refs[REACH + 5 : REACH + 12]
    q_turned, g_turned, q_rows, g_rows, scores, shares, out_sum, dq_sum = refs[
        REACH + 12 : REACH + 20
    ]
    q_sem, kv_sem, out_sem, grad_sem = refs[REACH + 20 :]
    step = pl.program_id(0)
    head = lax.div(step, 2)
    later = lax.rem(step, 2)
    core = meta[2]
    count = jnp.where(later == 1, meta[1], meta[0])
    groups = lax.div(count + GROUP - 1, GROUP)
    offset = 1 - later

    def wide_cols(j):
        return pl.ds(pl.multiple_of(j * WIDE, WIDE), WIDE)

    def fetch_rows(i, own):
        pairs = ((q_own, q_got, q_in), (g_own, g_got, g_in))
        return [
            pltpu.make_async_copy(
                mine.at[relay, 0, :, wide_cols(HEADS * core + i // 2)]
                if own
                else got.at[relay, :, pl.ds((i // 2) * WIDE, WIDE)],
                to.at[i],
                q_sem.at[k, i],
            )
            for k, (mine, got, to) in enumerate(pairs)
        ]

    def fetch_keys(j, distance):
        return pltpu.make_async_copy(
            pieces[distance].at[:, :, :, pl.ds(j * HEAD_WIDTH, HEAD_WIDTH)],
            kv.at[j, :, pl.ds(2 * distance, 2)],
            kv_sem.at[j, distance],
        )

    def give_rows(i, own):
        return [
            pltpu.make_async_copy(
                source.at[i],
                target.at[relay, 0, :, wide_cols(HEADS * core + i // 2)]
                if own
                else out_send.at[k, :, pl.ds((i // 2) * WIDE, WIDE)],
                out_sem.at[k, i],
            )
            for k, (source, target) in enumerate(((o_out, o_ref), (dq_out, dq_ref)))
        ]

    def give_grads(j, distance):
        return pltpu.make_async_copy(
            grads_low.at[j, :, pl.ds(2 * distance, 2)],
            terms[distance].at[:, :, :, pl.ds(j * HEAD_WIDTH, HEAD_WIDTH)],
            grad_sem.at[j, distance],
        )

    def start_all(copies):
        for copy in copies:
            copy.start()

    def wait_all(copies):
        for copy in copies:
            copy.wait()

    @pl.when(step == 0)
    def _():
        for i in range(STEPS):
            pl.when(core == i % 2)(lambda: start_all(fetch_rows(i, True)))
            pl.when(core != i % 2)(lambda: start_all(fetch_rows(i, False)))
            if i % 2 == 0:
                start_all(fetch_keys(i // 2, distance) for distance in range(REACH + 1))

    for i in range(STEPS):

        @pl.when(step == i)
        def _():
            wait_all(fetch_rows(i, False))
            if i % 2 == 0:
                wait_all(fetch_keys(i // 2, distance) for distance in range(REACH + 1))

    heads = [slice(i * HEAD_WIDTH, (i + 1) * HEAD_WIDTH) for i in range(QUERY_PER_KV)]
    for part in heads:
        q, g = q_in[step, :, part], g_in[step, :, part]
        q_rows[part, :] = q
        g_rows[part, :] = g
        q_turned[:, part] = q.T
        g_turned[:, part] = g.T

    def tiles_of(which, group):
        rows = kv[head, which, pl.ds(offset + group * GROUP, GROUP)]
        return rows.reshape(GROUP * TILE, HEAD_WIDTH)

    def block(group):
        return pl.ds(pl.multiple_of(group * GROUP * TILE, GROUP * TILE), GROUP * TILE)

    def scores_of(group):
        score = dot(tiles_of(0, group), q_turned[...], 1, 0)
        rows = [score[:TILE]]
        for i in range(1, GROUP):
            bias = jnp.where(GROUP * group + i < count, 0.0, HIDDEN).astype(jnp.float32)
            rows.append(score[i * TILE : (i + 1) * TILE] + bias)
        return rows

    def keep_scores(group, rows, top):
        score = jnp.concatenate(rows, axis=0)
        scores[block(group), :] = score
        most = jnp.max(score.reshape(-1, 8, ROWS), axis=0)
        return most if top is None else jnp.maximum(top, most)

    row = lax.broadcasted_iota(jnp.int32, (TILE, TILE), 0)
    column = lax.broadcasted_iota(jnp.int32, (TILE, TILE), 1)
    seen = jnp.concatenate([row <= column] * QUERY_PER_KV, axis=1)
    rows = scores_of(0)
    top = keep_scores(0, [jnp.where(seen, rows[0], HIDDEN)] + rows[1:], None)
    top = lax.fori_loop(
        1, groups, lambda group, top: keep_scores(group, scores_of(group), top), top
    )
    logit = jnp.concatenate(
        [
            jnp.full(
                (1, TILE), sink[(HEADS * core + head) * QUERY_PER_KV + i] * LOG2E, jnp.float32
            )
            for i in range(QUERY_PER_KV)
        ],
        axis=1,
    )
    top = jnp.maximum(jnp.max(top, axis=0, keepdims=True) * (SCALE * LOG2E), logit)

    out_sum[...] = jnp.zeros_like(out_sum)
    dq_sum[...] = jnp.zeros_like(dq_sum)
    ones = jnp.ones((16, GROUP * TILE), jnp.bfloat16)

    def share_step(group, carry):
        turned = jnp.concatenate([tiles_of(1, group).T, ones], axis=0)
        low = jnp.exp2(scores[block(group), :] * (SCALE * LOG2E) - top).astype(jnp.bfloat16)
        shares[block(group), :] = low
        out_sum[...] += dot(turned, low, 1, 0)
        return carry

    lax.fori_loop(0, groups, share_step, 0)
    sink_raised = jnp.exp2(logit - top)
    inverse = 1.0 / (out_sum[HEAD_WIDTH : HEAD_WIDTH + 1, :] + sink_raised)
    out = (out_sum[:HEAD_WIDTH, :] * inverse).astype(jnp.bfloat16)
    delta = jnp.sum(
        out.astype(jnp.float32) * g_turned[...].astype(jnp.float32), axis=0, keepdims=True
    )
    sink_rows = sink_raised * inverse * delta
    for i, part in enumerate(heads):
        o_out[step, :, part] = out[:, part].T
        sink_part[0, i : i + 1, :] = jnp.broadcast_to(
            -jnp.sum(sink_rows[:, part], axis=1, keepdims=True), (1, HEAD_WIDTH)
        )

    @pl.when(later == 0)
    def _():
        grads[...] = jnp.zeros_like(grads)

    def add_grads(which, group, term):
        rows = pl.ds(offset + group * GROUP, GROUP)
        grads[which, rows] += term.reshape(GROUP, TILE, HEAD_WIDTH)

    def grad_step(group, carry):
        share = shares[block(group), :].astype(jnp.float32) * inverse
        share_grad = dot(tiles_of(1, group), g_turned[...], 1, 0)
        score_grad = (share * (share_grad - delta)).astype(jnp.bfloat16)
        dq_sum[...] += dot(tiles_of(0, group).T, score_grad, 1, 0)
        add_grads(0, group, dot(score_grad, q_rows[...], 1, 0))
        add_grads(1, group, dot(share.astype(jnp.bfloat16), g_rows[...], 1, 0))
        return carry

    lax.fori_loop(0, groups, grad_step, 0)
    for part in heads:
        dq_out[step, :, part] = (dq_sum[:, part] * SCALE).astype(jnp.bfloat16).T

    @pl.when(later == 1)
    def _():
        grads_low[head, 0] = (grads[0] * SCALE).astype(jnp.bfloat16)
        grads_low[head, 1] = grads[1].astype(jnp.bfloat16)

    for i in range(STEPS):

        @pl.when(step == i)
        def _():
            pl.when(core == i % 2)(lambda: start_all(give_rows(i, True)))
            pl.when(core != i % 2)(lambda: start_all(give_rows(i, False)))
            if i % 2 == 1:
                start_all(give_grads(i // 2, distance) for distance in range(REACH + 1))

    @pl.when(step == STEPS - 1)
    def _():
        for i in range(STEPS):
            wait_all(give_rows(i, False))
            if i % 2 == 1:
                wait_all(give_grads(i // 2, distance) for distance in range(REACH + 1))


def attend(relay, meta, sink, queries, output_gradient, got, pieces, filled):
    smem = pl.BlockSpec(memory_space=pltpu.SMEM)
    whole = pl.BlockSpec(memory_space=pl.ANY)
    low = jnp.bfloat16
    inputs = [queries, output_gradient, *got, *pieces, *filled]
    first = 2 + len(inputs) - len(filled)
    rows = pltpu.VMEM((STEPS, TILE, WIDE), low)
    return pl.pallas_call(
        functools.partial(attend_kernel, relay, len(filled)),
        grid=(STEPS,),
        in_specs=[smem, smem] + [whole] * len(inputs),
        out_specs=[whole] * (REACH + 4)
        + [pl.BlockSpec((1, QUERY_PER_KV, HEAD_WIDTH), lambda i: (i, 0, 0))],
        out_shape=[
            jax.ShapeDtypeStruct(queries.shape, low),
            jax.ShapeDtypeStruct(queries.shape, low),
            jax.ShapeDtypeStruct((2, TILE, QUERY_PART), low),
        ]
        + [jax.ShapeDtypeStruct((2, 2, TILE, KEY_PART), low)] * (REACH + 1)
        + [jax.ShapeDtypeStruct((STEPS, QUERY_PER_KV, HEAD_WIDTH), jnp.float32)],
        scratch_shapes=[
            rows,
            rows,
            rows,
            rows,
            pltpu.VMEM((HEADS, 2, SLOTS, TILE, HEAD_WIDTH), low),
            pltpu.VMEM((2, SLOTS, TILE, HEAD_WIDTH), jnp.float32),
            pltpu.VMEM((HEADS, 2, SLOTS, TILE, HEAD_WIDTH), low),
            pltpu.VMEM((HEAD_WIDTH, ROWS), low),
            pltpu.VMEM((HEAD_WIDTH, ROWS), low),
            pltpu.VMEM((ROWS, HEAD_WIDTH), low),
            pltpu.VMEM((ROWS, HEAD_WIDTH), low),
            pltpu.VMEM((LONGEST * TILE, ROWS), jnp.float32),
            pltpu.VMEM((LONGEST * TILE, ROWS), low),
            pltpu.VMEM((HEAD_WIDTH + 16, ROWS), jnp.float32),
            pltpu.VMEM((HEAD_WIDTH, ROWS), jnp.float32),
            pltpu.SemaphoreType.DMA((2, STEPS)),
            pltpu.SemaphoreType.DMA((HEADS, REACH + 1)),
            pltpu.SemaphoreType.DMA((2, STEPS)),
            pltpu.SemaphoreType.DMA((HEADS, REACH + 1)),
        ],
        input_output_aliases={first + i: i for i in range(len(filled))},
        compiler_params=pltpu.CompilerParams(vmem_limit_bytes=VMEM_BYTES),
        cost_estimate=pl.CostEstimate(
            flops=12 * LONGEST * HQ * TILE * TILE * HEAD_WIDTH * 4,
            bytes_accessed=9 << 20,
            transcendentals=LONGEST * HQ * TILE * TILE,
        ),
        name=f"attend_{relay}",
    )(meta, sink, *inputs)


def shards(queries, keys, values, output_gradient, doc_tiles, sink_logits):
    ctx_count = lax.axis_size("ctx")
    ctx_pos = lax.axis_index("ctx")
    section_pos = lax.axis_index("section")
    section_count = lax.axis_size("section")
    core = lax.rem(ctx_pos, 2)
    first, second = 1, 0

    def shifted(pieces, amount):
        route = [
            (c, c + amount * 2 * (distance + 1))
            for distance in range(REACH)
            for c in range(ctx_count)
        ]
        routes = [route[d * ctx_count : (d + 1) * ctx_count] for d in range(REACH)]
        return [
            lax.ppermute(
                pieces[d + 1] if len(pieces) > 1 else pieces[0],
                "ctx",
                [(a, b) for a, b in routes[d] if 0 <= b < ctx_count],
            )
            for d in range(REACH)
        ]

    def swapped(array):
        return lax.ppermute(array, "ctx", [(c, c ^ 1) for c in range(ctx_count)])

    def half(array, which):
        width = array.shape[-1] // 2
        return lax.dynamic_slice_in_dim(array, which * width, width, array.ndim - 1)

    def in_order(own, got, later_first, axis):
        own_first = (core == 1) if later_first else (core == 0)
        return jnp.stack(
            [jnp.where(own_first, own, got), jnp.where(own_first, got, own)], axis=axis
        )

    def meta_of(relay):
        counts = []
        for position in (ctx_pos - core, ctx_pos - core + 1):
            end = start = jnp.zeros((), jnp.int32)
            for document in range(DOCS):
                end = end + doc_tiles[relay, 0, document]
                start = jnp.where(end <= position, end, start)
            counts.append(position - start + 1)
        return jnp.stack(counts + [core]).astype(jnp.int32)

    def sink_of(relay):
        layer = section_pos if relay == 0 else section_count - 1 - section_pos
        return lax.dynamic_index_in_dim(sink_logits, layer, 0, keepdims=False)

    def sink_terms(sink_part):
        mine = jnp.sum(sink_part[:, :, 0].reshape(HEADS, 2, QUERY_PER_KV), axis=1).reshape(-1)
        mine = jnp.concatenate([mine, mine])
        return jnp.where(jnp.arange(HQ) // (HQ // 2) == core, mine, 0.0)

    def summed(terms, sent):
        total = terms[0].astype(jnp.float32)
        for other in sent:
            total = total + other.astype(jnp.float32)
        return total.astype(jnp.bfloat16)

    both = jnp.stack([keys[:, 0], values[:, 0]], axis=1)
    own = half(both, core)
    piece = in_order(own, swapped(half(both, 1 - core)), True, 2)
    pieces = [piece[relay] for relay in range(RELAY_COUNT)]
    pieces[0], pieces[1], mate = lax.optimization_barrier((pieces[0], pieces[1], 1 - core))
    mine_first = [pieces[first]] + shifted([pieces[first]], 1)
    got = [swapped(half(array[:, 0], mate)) for array in (queries, output_gradient)]
    mine_second = [pieces[second]] + shifted([pieces[second]], 1)
    attention, query_grad, out_first, *terms_first, sink_part = attend(
        first, meta_of(first), sink_of(first), queries, output_gradient, got, mine_first, []
    )
    mine_second, sink_part = lax.optimization_barrier((mine_second, sink_part))
    sent_first = shifted(terms_first, -1)
    out_first = swapped(out_first)
    mirrored = lax.ppermute(
        sink_terms(sink_part),
        "section",
        [(s, section_count - 1 - s) for s in range(section_count)],
    )
    attention, query_grad, out_second, *terms_second, sink_part = attend(
        second,
        meta_of(second),
        sink_of(second),
        queries,
        output_gradient,
        got,
        mine_second,
        [attention, query_grad],
    )
    sent_first, out_first, mirrored, sink_part = lax.optimization_barrier(
        (sent_first, out_first, mirrored, sink_part)
    )
    sent_second = shifted(terms_second, -1)
    out_second = swapped(out_second)
    sink_grad = sink_terms(sink_part) + mirrored
    distance = 1
    while distance < ctx_count:
        sink_grad = sink_grad + lax.ppermute(
            sink_grad, "ctx", [(c, c ^ distance) for c in range(ctx_count)]
        )
        distance *= 2
    for relay, got in ((first, out_first), (second, out_second)):
        place = (relay, 0, 0, mate * QUERY_PART)
        attention = lax.dynamic_update_slice(attention, got[0][None, None], place)
        query_grad = lax.dynamic_update_slice(query_grad, got[1][None, None], place)
    first_sum = summed(terms_first, sent_first)
    sent_second, sink_grad, first_sum, attention, query_grad = lax.optimization_barrier(
        (sent_second, sink_grad, first_sum, attention, query_grad)
    )
    second_sum = summed(terms_second, sent_second)
    sums = jnp.stack([second_sum, first_sum])
    own = lax.dynamic_index_in_dim(sums, mate, 2, keepdims=False)
    got = swapped(lax.dynamic_index_in_dim(sums, core, 2, keepdims=False))
    grads = jnp.concatenate(
        [jnp.where(core == 0, own, got), jnp.where(core == 0, got, own)], axis=-1
    )
    return (attention, query_grad, grads[:, :1], grads[:, 1:], sink_grad[None])


def solution(mesh):
    placed = (
        P(None, "section", "ctx", None),
        P(None, "section", "ctx", None),
        P(None, "section", "ctx", None),
        P(None, "section", "ctx", None),
        P(None, "section", None),
        P(),
    )
    return jax.shard_map(
        shards,
        mesh=mesh,
        in_specs=placed,
        out_specs=(
            P(None, "section", "ctx", None),
            P(None, "section", "ctx", None),
            P(None, "section", "ctx", None),
            P(None, "section", "ctx", None),
            P("section", None),
        ),
        check_vma=False,
    )
```

```python
import functools
import math

import jax
import jax.numpy as jnp
from jax import lax
from jax.experimental import pallas as pl
from jax.experimental.pallas import tpu as pltpu
from jax.sharding import PartitionSpec as P

HEAD_WIDTH = 128
HQ = 32
KEY_HEADS = 4
QUERY_PER_KV = 8
TILE = 128
DOCS = 4
RELAY_COUNT = 2
LONGEST = 9
REACH = LONGEST // 2
ROWS = QUERY_PER_KV * TILE
SCALE = 1.0 / math.sqrt(HEAD_WIDTH)
LOG2E = 1.4426950408889634
HIDDEN = -1e30
VMEM_BYTES = 20 * 1024 * 1024
GROUP = 3
SLOTS = 2 * (REACH + 1)
HEADS = KEY_HEADS // 2
STEPS = 2 * HEADS
KEY_PART = HEADS * HEAD_WIDTH
WIDE = QUERY_PER_KV * HEAD_WIDTH
QUERY_PART = HEADS * WIDE


def dot(left, right, left_dim, right_dim):
    return lax.dot_general(
        left,
        right,
        (((left_dim,), (right_dim,)), ((), ())),
        preferred_element_type=jnp.float32,
    )


def attend_kernel(relay, refilled, doc_tiles, sink, q_own, g_own, q_got, g_got, *refs):
    pieces = refs[: REACH + 1]
    refs = refs[REACH + 1 + refilled :]
    o_ref, dq_ref, out_send = refs[:3]
    terms = refs[3 : REACH + 4]
    sink_part = refs[REACH + 4]
    q_in, g_in, o_out, dq_out, kv, grads, grads_low = refs[REACH + 5 : REACH + 12]
    q_turned, g_turned, q_rows, g_rows, scores, shares, out_sum, dq_sum = refs[
        REACH + 12 : REACH + 20
    ]
    q_sem, kv_sem, out_sem, grad_sem = refs[REACH + 20 :]
    step = pl.program_id(0)
    head = lax.div(step, 2)
    later = lax.rem(step, 2)
    ctx_pos = lax.axis_index("ctx")
    section_pos = lax.axis_index("section")
    core = lax.rem(ctx_pos, 2)
    layer = section_pos if relay == 0 else lax.axis_size("section") - 1 - section_pos
    position = ctx_pos - core + later
    end = start = jnp.int32(0)
    for document in range(DOCS):
        end = end + doc_tiles[relay, 0, document]
        start = jnp.where(end <= position, end, start)
    count = position - start + 1
    groups = lax.div(count + GROUP - 1, GROUP)
    offset = 1 - later

    def wide_cols(j):
        return pl.ds(pl.multiple_of(j * WIDE, WIDE), WIDE)

    def fetch_rows(i, own):
        pairs = ((q_own, q_got, q_in), (g_own, g_got, g_in))
        return [
            pltpu.make_async_copy(
                mine.at[relay, 0, :, wide_cols(HEADS * core + i // 2)]
                if own
                else got.at[relay, :, pl.ds((i // 2) * WIDE, WIDE)],
                to.at[i],
                q_sem.at[k, i],
            )
            for k, (mine, got, to) in enumerate(pairs)
        ]

    def fetch_keys(j, distance):
        return pltpu.make_async_copy(
            pieces[distance].at[:, :, :, pl.ds(j * HEAD_WIDTH, HEAD_WIDTH)],
            kv.at[j, :, pl.ds(2 * distance, 2)],
            kv_sem.at[j, distance],
        )

    def give_rows(i, own):
        return [
            pltpu.make_async_copy(
                source.at[i],
                target.at[relay, 0, :, wide_cols(HEADS * core + i // 2)]
                if own
                else out_send.at[k, :, pl.ds((i // 2) * WIDE, WIDE)],
                out_sem.at[k, i],
            )
            for k, (source, target) in enumerate(((o_out, o_ref), (dq_out, dq_ref)))
        ]

    def give_grads(j, distance):
        return pltpu.make_async_copy(
            grads_low.at[j, :, pl.ds(2 * distance, 2)],
            terms[distance].at[:, :, :, pl.ds(j * HEAD_WIDTH, HEAD_WIDTH)],
            grad_sem.at[j, distance],
        )

    def start_all(copies):
        for copy in copies:
            copy.start()

    def wait_all(copies):
        for copy in copies:
            copy.wait()

    @pl.when(step == 0)
    def _():
        for i in range(STEPS):
            pl.when(core == i % 2)(lambda: start_all(fetch_rows(i, True)))
            pl.when(core != i % 2)(lambda: start_all(fetch_rows(i, False)))
            if i % 2 == 0:
                start_all(fetch_keys(i // 2, distance) for distance in range(REACH + 1))

    for i in range(STEPS):

        @pl.when(step == i)
        def _():
            wait_all(fetch_rows(i, False))
            if i % 2 == 0:
                wait_all(fetch_keys(i // 2, distance) for distance in range(REACH + 1))

    heads = [slice(i * HEAD_WIDTH, (i + 1) * HEAD_WIDTH) for i in range(QUERY_PER_KV)]
    for part in heads:
        q, g = q_in[step, :, part], g_in[step, :, part]
        q_rows[part, :] = q
        g_rows[part, :] = g
        q_turned[:, part] = q.T
        g_turned[:, part] = g.T

    def tiles_of(which, group):
        rows = kv[head, which, pl.ds(offset + group * GROUP, GROUP)]
        return rows.reshape(GROUP * TILE, HEAD_WIDTH)

    def block(group):
        return pl.ds(pl.multiple_of(group * GROUP * TILE, GROUP * TILE), GROUP * TILE)

    def scores_of(group):
        score = dot(tiles_of(0, group), q_turned[...], 1, 0)
        rows = [score[:TILE]]
        for i in range(1, GROUP):
            bias = jnp.where(GROUP * group + i < count, 0.0, HIDDEN).astype(jnp.float32)
            rows.append(score[i * TILE : (i + 1) * TILE] + bias)
        return rows

    def keep_scores(group, rows, top):
        score = jnp.concatenate(rows, axis=0)
        scores[block(group), :] = score
        most = jnp.max(score.reshape(-1, 8, ROWS), axis=0)
        return most if top is None else jnp.maximum(top, most)

    row = lax.broadcasted_iota(jnp.int32, (TILE, TILE), 0)
    column = lax.broadcasted_iota(jnp.int32, (TILE, TILE), 1)
    seen = jnp.concatenate([row <= column] * QUERY_PER_KV, axis=1)
    rows = scores_of(0)
    top = keep_scores(0, [jnp.where(seen, rows[0], HIDDEN)] + rows[1:], None)
    top = lax.fori_loop(
        1, groups, lambda group, top: keep_scores(group, scores_of(group), top), top
    )
    logit = jnp.concatenate(
        [
            jnp.full(
                (1, TILE), sink[layer, (HEADS * core + head) * QUERY_PER_KV + i] * LOG2E, jnp.float32
            )
            for i in range(QUERY_PER_KV)
        ],
        axis=1,
    )
    top = jnp.maximum(jnp.max(top, axis=0, keepdims=True) * (SCALE * LOG2E), logit)

    out_sum[...] = jnp.zeros_like(out_sum)
    dq_sum[...] = jnp.zeros_like(dq_sum)
    ones = jnp.ones((16, GROUP * TILE), jnp.bfloat16)

    def share_step(group, carry):
        turned = jnp.concatenate([tiles_of(1, group).T, ones], axis=0)
        low = jnp.exp2(scores[block(group), :] * (SCALE * LOG2E) - top).astype(jnp.bfloat16)
        shares[block(group), :] = low
        out_sum[...] += dot(turned, low, 1, 0)
        return carry

    lax.fori_loop(0, groups, share_step, 0)
    sink_raised = jnp.exp2(logit - top)
    inverse = 1.0 / (out_sum[HEAD_WIDTH : HEAD_WIDTH + 1, :] + sink_raised)
    out = (out_sum[:HEAD_WIDTH, :] * inverse).astype(jnp.bfloat16)
    delta = jnp.sum(
        out.astype(jnp.float32) * g_turned[...].astype(jnp.float32), axis=0, keepdims=True
    )
    sink_rows = sink_raised * inverse * delta
    for i, part in enumerate(heads):
        o_out[step, :, part] = out[:, part].T
        sink_part[0, i : i + 1, :] = jnp.broadcast_to(
            -jnp.sum(sink_rows[:, part], axis=1, keepdims=True), (1, HEAD_WIDTH)
        )

    @pl.when(later == 0)
    def _():
        grads[...] = jnp.zeros_like(grads)

    def add_grads(which, group, term):
        rows = pl.ds(offset + group * GROUP, GROUP)
        grads[which, rows] += term.reshape(GROUP, TILE, HEAD_WIDTH)

    def grad_step(group, carry):
        share = shares[block(group), :].astype(jnp.float32) * inverse
        share_grad = dot(tiles_of(1, group), g_turned[...], 1, 0)
        score_grad = (share * (share_grad - delta)).astype(jnp.bfloat16)
        dq_sum[...] += dot(tiles_of(0, group).T, score_grad, 1, 0)
        add_grads(0, group, dot(score_grad, q_rows[...], 1, 0))
        add_grads(1, group, dot(share.astype(jnp.bfloat16), g_rows[...], 1, 0))
        return carry

    lax.fori_loop(0, groups, grad_step, 0)
    for part in heads:
        dq_out[step, :, part] = (dq_sum[:, part] * SCALE).astype(jnp.bfloat16).T

    @pl.when(later == 1)
    def _():
        grads_low[head, 0] = (grads[0] * SCALE).astype(jnp.bfloat16)
        grads_low[head, 1] = grads[1].astype(jnp.bfloat16)

    for i in range(STEPS):

        @pl.when(step == i)
        def _():
            pl.when(core == i % 2)(lambda: start_all(give_rows(i, True)))
            pl.when(core != i % 2)(lambda: start_all(give_rows(i, False)))
            if i % 2 == 1:
                start_all(give_grads(i // 2, distance) for distance in range(REACH + 1))

    @pl.when(step == STEPS - 1)
    def _():
        for i in range(STEPS):
            wait_all(give_rows(i, False))
            if i % 2 == 1:
                wait_all(give_grads(i // 2, distance) for distance in range(REACH + 1))


def attend(relay, doc_tiles, sink_logits, queries, output_gradient, got, pieces, filled):
    smem = pl.BlockSpec(memory_space=pltpu.SMEM)
    whole = pl.BlockSpec(memory_space=pl.ANY)
    low = jnp.bfloat16
    inputs = [queries, output_gradient, *got, *pieces, *filled]
    first = 2 + len(inputs) - len(filled)
    rows = pltpu.VMEM((STEPS, TILE, WIDE), low)
    return pl.pallas_call(
        functools.partial(attend_kernel, relay, len(filled)),
        grid=(STEPS,),
        in_specs=[smem, smem] + [whole] * len(inputs),
        out_specs=[whole] * (REACH + 4)
        + [pl.BlockSpec((1, QUERY_PER_KV, HEAD_WIDTH), lambda i: (i, 0, 0))],
        out_shape=[
            jax.ShapeDtypeStruct(queries.shape, low),
            jax.ShapeDtypeStruct(queries.shape, low),
            jax.ShapeDtypeStruct((2, TILE, QUERY_PART), low),
        ]
        + [jax.ShapeDtypeStruct((2, 2, TILE, KEY_PART), low)] * (REACH + 1)
        + [jax.ShapeDtypeStruct((STEPS, QUERY_PER_KV, HEAD_WIDTH), jnp.float32)],
        scratch_shapes=[
            rows,
            rows,
            rows,
            rows,
            pltpu.VMEM((HEADS, 2, SLOTS, TILE, HEAD_WIDTH), low),
            pltpu.VMEM((2, SLOTS, TILE, HEAD_WIDTH), jnp.float32),
            pltpu.VMEM((HEADS, 2, SLOTS, TILE, HEAD_WIDTH), low),
            pltpu.VMEM((HEAD_WIDTH, ROWS), low),
            pltpu.VMEM((HEAD_WIDTH, ROWS), low),
            pltpu.VMEM((ROWS, HEAD_WIDTH), low),
            pltpu.VMEM((ROWS, HEAD_WIDTH), low),
            pltpu.VMEM((LONGEST * TILE, ROWS), jnp.float32),
            pltpu.VMEM((LONGEST * TILE, ROWS), low),
            pltpu.VMEM((HEAD_WIDTH + 16, ROWS), jnp.float32),
            pltpu.VMEM((HEAD_WIDTH, ROWS), jnp.float32),
            pltpu.SemaphoreType.DMA((2, STEPS)),
            pltpu.SemaphoreType.DMA((HEADS, REACH + 1)),
            pltpu.SemaphoreType.DMA((2, STEPS)),
            pltpu.SemaphoreType.DMA((HEADS, REACH + 1)),
        ],
        input_output_aliases={first + i: i for i in range(len(filled))},
        compiler_params=pltpu.CompilerParams(vmem_limit_bytes=VMEM_BYTES),
        cost_estimate=pl.CostEstimate(
            flops=12 * LONGEST * HQ * TILE * TILE * HEAD_WIDTH * 4,
            bytes_accessed=9 << 20,
            transcendentals=LONGEST * HQ * TILE * TILE,
        ),
        name=f"attend_{relay}",
    )(doc_tiles, sink_logits, *inputs)


def shards(queries, keys, values, output_gradient, doc_tiles, sink_logits):
    ctx_count = lax.axis_size("ctx")
    ctx_pos = lax.axis_index("ctx")
    section_pos = lax.axis_index("section")
    section_count = lax.axis_size("section")
    core = lax.rem(ctx_pos, 2)
    first, second = 1, 0

    def shifted(pieces, amount):
        route = [
            (c, c + amount * 2 * (distance + 1))
            for distance in range(REACH)
            for c in range(ctx_count)
        ]
        routes = [route[d * ctx_count : (d + 1) * ctx_count] for d in range(REACH)]
        return [
            lax.ppermute(
                pieces[d + 1] if len(pieces) > 1 else pieces[0],
                "ctx",
                [(a, b) for a, b in routes[d] if 0 <= b < ctx_count],
            )
            for d in range(REACH)
        ]

    def swapped(array):
        return lax.ppermute(array, "ctx", [(c, c ^ 1) for c in range(ctx_count)])

    def half(array, which):
        width = array.shape[-1] // 2
        return lax.dynamic_slice_in_dim(array, which * width, width, array.ndim - 1)

    def in_order(own, got, later_first, axis):
        own_first = (core == 1) if later_first else (core == 0)
        return jnp.stack(
            [jnp.where(own_first, own, got), jnp.where(own_first, got, own)], axis=axis
        )

    def sink_terms(sink_part):
        mine = jnp.sum(sink_part[:, :, 0].reshape(HEADS, 2, QUERY_PER_KV), axis=1).reshape(-1)
        mine = jnp.concatenate([mine, mine])
        return jnp.where(jnp.arange(HQ) // (HQ // 2) == core, mine, 0.0)

    def summed(terms, sent):
        total = terms[0].astype(jnp.float32)
        for other in sent:
            total = total + other.astype(jnp.float32)
        return total.astype(jnp.bfloat16)

    def halves(which):
        return jnp.stack([half(keys[:, 0], which), half(values[:, 0], which)], axis=1)

    piece = in_order(halves(core), swapped(halves(1 - core)), True, 2)
    pieces = [piece[relay] for relay in range(RELAY_COUNT)]
    pieces[0], pieces[1], mate = lax.optimization_barrier((pieces[0], pieces[1], 1 - core))
    mine_first = [pieces[first]] + shifted([pieces[first]], 1)
    got = [swapped(half(array[:, 0], mate)) for array in (queries, output_gradient)]
    mine_second = [pieces[second]] + shifted([pieces[second]], 1)
    attention, query_grad, out_first, *terms_first, sink_part = attend(
        first, doc_tiles, sink_logits, queries, output_gradient, got, mine_first, []
    )
    mine_second, sink_part = lax.optimization_barrier((mine_second, sink_part))
    sent_first = shifted(terms_first, -1)
    out_first = swapped(out_first)
    sink_first = sink_terms(sink_part)
    attention, query_grad, out_second, *terms_second, sink_part = attend(
        second,
        doc_tiles,
        sink_logits,
        queries,
        output_gradient,
        got,
        mine_second,
        [attention, query_grad],
    )
    sent_first, out_first, sink_first, sink_part, out_second, terms_second = (
        lax.optimization_barrier(
            (sent_first, out_first, sink_first, sink_part, out_second, terms_second)
        )
    )
    sent_second = shifted(terms_second, -1)
    out_second = swapped(out_second)
    out_second, sink_first = lax.optimization_barrier((out_second, sink_first))
    sink_grad = sink_terms(sink_part) + lax.ppermute(
        sink_first,
        "section",
        [(s, section_count - 1 - s) for s in range(section_count)],
    )
    distance = 1
    while distance < ctx_count:
        sink_grad = sink_grad + lax.ppermute(
            sink_grad, "ctx", [(c, c ^ distance) for c in range(ctx_count)]
        )
        distance *= 2
    for relay, got in ((first, out_first), (second, out_second)):
        place = (relay, 0, 0, mate * QUERY_PART)
        attention = lax.dynamic_update_slice(attention, got[0][None, None], place)
        query_grad = lax.dynamic_update_slice(query_grad, got[1][None, None], place)
    first_sum = summed(terms_first, sent_first)
    sent_second, sink_grad, first_sum, attention, query_grad = lax.optimization_barrier(
        (sent_second, sink_grad, first_sum, attention, query_grad)
    )
    second_sum = summed(terms_second, sent_second)
    sums = jnp.stack([second_sum, first_sum])
    own = lax.dynamic_index_in_dim(sums, mate, 2, keepdims=False)
    got = swapped(lax.dynamic_index_in_dim(sums, core, 2, keepdims=False))
    grads = jnp.concatenate(
        [jnp.where(core == 0, own, got), jnp.where(core == 0, got, own)], axis=-1
    )
    return (attention, query_grad, grads[:, :1], grads[:, 1:], sink_grad[None])


def solution(mesh):
    placed = (
        P(None, "section", "ctx", None),
        P(None, "section", "ctx", None),
        P(None, "section", "ctx", None),
        P(None, "section", "ctx", None),
        P(None, "section", None),
        P(),
    )
    return jax.shard_map(
        shards,
        mesh=mesh,
        in_specs=placed,
        out_specs=(
            P(None, "section", "ctx", None),
            P(None, "section", "ctx", None),
            P(None, "section", "ctx", None),
            P(None, "section", "ctx", None),
            P("section", None),
        ),
        check_vma=False,
    )
```

```python
import functools
import math

import jax
import jax.numpy as jnp
from jax import lax
from jax.experimental import pallas as pl
from jax.experimental.pallas import tpu as pltpu
from jax.sharding import PartitionSpec as P

HEAD_WIDTH = 128
HQ = 32
KEY_HEADS = 4
QUERY_PER_KV = 8
TILE = 128
DOCS = 4
RELAY_COUNT = 2
LONGEST = 9
REACH = LONGEST // 2
ROWS = QUERY_PER_KV * TILE
SCALE = 1.0 / math.sqrt(HEAD_WIDTH)
LOG2E = 1.4426950408889634
HIDDEN = -1e30
VMEM_BYTES = 20 * 1024 * 1024
GROUP = 3
SLOTS = 2 * (REACH + 1)
HEADS = KEY_HEADS // 2
STEPS = 2 * HEADS
KEY_PART = HEADS * HEAD_WIDTH
WIDE = QUERY_PER_KV * HEAD_WIDTH
QUERY_PART = HEADS * WIDE


def dot(left, right, left_dim, right_dim):
    return lax.dot_general(
        left,
        right,
        (((left_dim,), (right_dim,)), ((), ())),
        preferred_element_type=jnp.float32,
    )


def attend_kernel(relay, refilled, doc_tiles, sink, q_own, g_own, got, *refs):
    pieces = refs[: REACH + 1]
    refs = refs[REACH + 1 + refilled :]
    o_ref, dq_ref, out_send = refs[:3]
    terms = refs[3 : REACH + 4]
    sink_part = refs[REACH + 4]
    q_in, g_in, o_out, dq_out, kv, grads, grads_low = refs[REACH + 5 : REACH + 12]
    q_turned, g_turned, q_rows, g_rows, scores, shares, out_sum, dq_sum = refs[
        REACH + 12 : REACH + 20
    ]
    q_sem, kv_sem, out_sem, grad_sem = refs[REACH + 20 :]
    step = pl.program_id(0)
    head = lax.div(step, 2)
    later = lax.rem(step, 2)
    ctx_pos = lax.axis_index("ctx")
    section_pos = lax.axis_index("section")
    core = lax.rem(ctx_pos, 2)
    layer = section_pos if relay == 0 else lax.axis_size("section") - 1 - section_pos
    position = ctx_pos - core + later
    end = start = jnp.int32(0)
    for document in range(DOCS):
        end = end + doc_tiles[relay, 0, document]
        start = jnp.where(end <= position, end, start)
    count = position - start + 1
    groups = lax.div(count + GROUP - 1, GROUP)
    offset = 1 - later

    def wide_cols(j):
        return pl.ds(pl.multiple_of(j * WIDE, WIDE), WIDE)

    def fetch_rows(i, own):
        pairs = ((q_own, q_in), (g_own, g_in))
        return [
            pltpu.make_async_copy(
                mine.at[relay, 0, :, wide_cols(HEADS * core + i // 2)]
                if own
                else got.at[k, relay, :, pl.ds((i // 2) * WIDE, WIDE)],
                to.at[i],
                q_sem.at[k, i],
            )
            for k, (mine, to) in enumerate(pairs)
        ]

    def fetch_keys(j, distance):
        return pltpu.make_async_copy(
            pieces[distance].at[:, :, :, pl.ds(j * HEAD_WIDTH, HEAD_WIDTH)],
            kv.at[j, :, pl.ds(2 * distance, 2)],
            kv_sem.at[j, distance],
        )

    def give_rows(i, own):
        return [
            pltpu.make_async_copy(
                source.at[i],
                target.at[relay, 0, :, wide_cols(HEADS * core + i // 2)]
                if own
                else out_send.at[relay, k, :, pl.ds((i // 2) * WIDE, WIDE)],
                out_sem.at[k, i],
            )
            for k, (source, target) in enumerate(((o_out, o_ref), (dq_out, dq_ref)))
        ]

    def give_grads(j, distance):
        return pltpu.make_async_copy(
            grads_low.at[j, :, pl.ds(2 * distance, 2)],
            terms[distance].at[:, :, :, pl.ds(j * HEAD_WIDTH, HEAD_WIDTH)],
            grad_sem.at[j, distance],
        )

    def start_all(copies):
        for copy in copies:
            copy.start()

    def wait_all(copies):
        for copy in copies:
            copy.wait()

    @pl.when(step == 0)
    def _():
        for i in range(STEPS):
            pl.when(core == i % 2)(lambda: start_all(fetch_rows(i, True)))
            pl.when(core != i % 2)(lambda: start_all(fetch_rows(i, False)))
            if i % 2 == 0:
                start_all(fetch_keys(i // 2, distance) for distance in range(REACH + 1))

    for i in range(STEPS):

        @pl.when(step == i)
        def _():
            wait_all(fetch_rows(i, False))
            if i % 2 == 0:
                wait_all(fetch_keys(i // 2, distance) for distance in range(REACH + 1))

    heads = [slice(i * HEAD_WIDTH, (i + 1) * HEAD_WIDTH) for i in range(QUERY_PER_KV)]
    for part in heads:
        q, g = q_in[step, :, part], g_in[step, :, part]
        q_rows[part, :] = q
        g_rows[part, :] = g
        q_turned[:, part] = q.T
        g_turned[:, part] = g.T

    def tiles_of(which, group):
        rows = kv[head, which, pl.ds(offset + group * GROUP, GROUP)]
        return rows.reshape(GROUP * TILE, HEAD_WIDTH)

    def block(group):
        return pl.ds(pl.multiple_of(group * GROUP * TILE, GROUP * TILE), GROUP * TILE)

    def scores_of(group):
        score = dot(tiles_of(0, group), q_turned[...], 1, 0)
        rows = [score[:TILE]]
        for i in range(1, GROUP):
            bias = jnp.where(GROUP * group + i < count, 0.0, HIDDEN).astype(jnp.float32)
            rows.append(score[i * TILE : (i + 1) * TILE] + bias)
        return rows

    def keep_scores(group, rows, top):
        score = jnp.concatenate(rows, axis=0)
        scores[block(group), :] = score
        most = jnp.max(score.reshape(-1, 8, ROWS), axis=0)
        return most if top is None else jnp.maximum(top, most)

    row = lax.broadcasted_iota(jnp.int32, (TILE, TILE), 0)
    column = lax.broadcasted_iota(jnp.int32, (TILE, TILE), 1)
    seen = jnp.concatenate([row <= column] * QUERY_PER_KV, axis=1)
    rows = scores_of(0)
    top = keep_scores(0, [jnp.where(seen, rows[0], HIDDEN)] + rows[1:], None)
    top = lax.fori_loop(
        1, groups, lambda group, top: keep_scores(group, scores_of(group), top), top
    )
    logit = jnp.concatenate(
        [
            jnp.full(
                (1, TILE), sink[layer, (HEADS * core + head) * QUERY_PER_KV + i] * LOG2E, jnp.float32
            )
            for i in range(QUERY_PER_KV)
        ],
        axis=1,
    )
    top = jnp.maximum(jnp.max(top, axis=0, keepdims=True) * (SCALE * LOG2E), logit)

    out_sum[...] = jnp.zeros_like(out_sum)
    dq_sum[...] = jnp.zeros_like(dq_sum)
    ones = jnp.ones((16, GROUP * TILE), jnp.bfloat16)

    def share_step(group, carry):
        turned = jnp.concatenate([tiles_of(1, group).T, ones], axis=0)
        low = jnp.exp2(scores[block(group), :] * (SCALE * LOG2E) - top).astype(jnp.bfloat16)
        shares[block(group), :] = low
        out_sum[...] += dot(turned, low, 1, 0)
        return carry

    lax.fori_loop(0, groups, share_step, 0)
    sink_raised = jnp.exp2(logit - top)
    inverse = 1.0 / (out_sum[HEAD_WIDTH : HEAD_WIDTH + 1, :] + sink_raised)
    out = (out_sum[:HEAD_WIDTH, :] * inverse).astype(jnp.bfloat16)
    delta = jnp.sum(
        out.astype(jnp.float32) * g_turned[...].astype(jnp.float32), axis=0, keepdims=True
    )
    sink_rows = sink_raised * inverse * delta
    for i, part in enumerate(heads):
        o_out[step, :, part] = out[:, part].T
        sink_part[0, i : i + 1, :] = jnp.broadcast_to(
            -jnp.sum(sink_rows[:, part], axis=1, keepdims=True), (1, HEAD_WIDTH)
        )

    @pl.when(later == 0)
    def _():
        grads[...] = jnp.zeros_like(grads)

    def add_grads(which, group, term):
        rows = pl.ds(offset + group * GROUP, GROUP)
        grads[which, rows] += term.reshape(GROUP, TILE, HEAD_WIDTH)

    def grad_step(group, carry):
        share = shares[block(group), :].astype(jnp.float32) * inverse
        share_grad = dot(tiles_of(1, group), g_turned[...], 1, 0)
        score_grad = (share * (share_grad - delta)).astype(jnp.bfloat16)
        dq_sum[...] += dot(tiles_of(0, group).T, score_grad, 1, 0)
        add_grads(0, group, dot(score_grad, q_rows[...], 1, 0))
        add_grads(1, group, dot(share.astype(jnp.bfloat16), g_rows[...], 1, 0))
        return carry

    lax.fori_loop(0, groups, grad_step, 0)
    for part in heads:
        dq_out[step, :, part] = (dq_sum[:, part] * SCALE).astype(jnp.bfloat16).T

    @pl.when(later == 1)
    def _():
        grads_low[head, 0] = (grads[0] * SCALE).astype(jnp.bfloat16)
        grads_low[head, 1] = grads[1].astype(jnp.bfloat16)

    for i in range(STEPS):

        @pl.when(step == i)
        def _():
            pl.when(core == i % 2)(lambda: start_all(give_rows(i, True)))
            pl.when(core != i % 2)(lambda: start_all(give_rows(i, False)))
            if i % 2 == 1:
                start_all(give_grads(i // 2, distance) for distance in range(REACH + 1))

    @pl.when(step == STEPS - 1)
    def _():
        for i in range(STEPS):
            wait_all(give_rows(i, False))
            if i % 2 == 1:
                wait_all(give_grads(i // 2, distance) for distance in range(REACH + 1))


def attend(relay, doc_tiles, sink_logits, queries, output_gradient, got, pieces, filled):
    smem = pl.BlockSpec(memory_space=pltpu.SMEM)
    whole = pl.BlockSpec(memory_space=pl.ANY)
    low = jnp.bfloat16
    inputs = [queries, output_gradient, got, *pieces, *filled]
    first = 2 + len(inputs) - len(filled)
    rows = pltpu.VMEM((STEPS, TILE, WIDE), low)
    return pl.pallas_call(
        functools.partial(attend_kernel, relay, len(filled)),
        grid=(STEPS,),
        in_specs=[smem, smem] + [whole] * len(inputs),
        out_specs=[whole] * (REACH + 4)
        + [pl.BlockSpec((1, QUERY_PER_KV, HEAD_WIDTH), lambda i: (i, 0, 0))],
        out_shape=[
            jax.ShapeDtypeStruct(queries.shape, low),
            jax.ShapeDtypeStruct(queries.shape, low),
            jax.ShapeDtypeStruct((RELAY_COUNT, 2, TILE, QUERY_PART), low),
        ]
        + [jax.ShapeDtypeStruct((2, 2, TILE, KEY_PART), low)] * (REACH + 1)
        + [jax.ShapeDtypeStruct((STEPS, QUERY_PER_KV, HEAD_WIDTH), jnp.float32)],
        scratch_shapes=[
            rows,
            rows,
            rows,
            rows,
            pltpu.VMEM((HEADS, 2, SLOTS, TILE, HEAD_WIDTH), low),
            pltpu.VMEM((2, SLOTS, TILE, HEAD_WIDTH), jnp.float32),
            pltpu.VMEM((HEADS, 2, SLOTS, TILE, HEAD_WIDTH), low),
            pltpu.VMEM((HEAD_WIDTH, ROWS), low),
            pltpu.VMEM((HEAD_WIDTH, ROWS), low),
            pltpu.VMEM((ROWS, HEAD_WIDTH), low),
            pltpu.VMEM((ROWS, HEAD_WIDTH), low),
            pltpu.VMEM((LONGEST * TILE, ROWS), jnp.float32),
            pltpu.VMEM((LONGEST * TILE, ROWS), low),
            pltpu.VMEM((HEAD_WIDTH + 16, ROWS), jnp.float32),
            pltpu.VMEM((HEAD_WIDTH, ROWS), jnp.float32),
            pltpu.SemaphoreType.DMA((2, STEPS)),
            pltpu.SemaphoreType.DMA((HEADS, REACH + 1)),
            pltpu.SemaphoreType.DMA((2, STEPS)),
            pltpu.SemaphoreType.DMA((HEADS, REACH + 1)),
        ],
        input_output_aliases={first + i: i for i in range(len(filled))},
        compiler_params=pltpu.CompilerParams(vmem_limit_bytes=VMEM_BYTES),
        cost_estimate=pl.CostEstimate(
            flops=12 * LONGEST * HQ * TILE * TILE * HEAD_WIDTH * 4,
            bytes_accessed=9 << 20,
            transcendentals=LONGEST * HQ * TILE * TILE,
        ),
        name=f"attend_{relay}",
    )(doc_tiles, sink_logits, *inputs)


def shards(queries, keys, values, output_gradient, doc_tiles, sink_logits):
    ctx_count = lax.axis_size("ctx")
    ctx_pos = lax.axis_index("ctx")
    section_pos = lax.axis_index("section")
    section_count = lax.axis_size("section")
    core = lax.rem(ctx_pos, 2)
    first, second = 1, 0

    def shifted(pieces, amount):
        route = [
            (c, c + amount * 2 * (distance + 1))
            for distance in range(REACH)
            for c in range(ctx_count)
        ]
        routes = [route[d * ctx_count : (d + 1) * ctx_count] for d in range(REACH)]
        return [
            lax.ppermute(
                pieces[d + 1] if len(pieces) > 1 else pieces[0],
                "ctx",
                [(a, b) for a, b in routes[d] if 0 <= b < ctx_count],
            )
            for d in range(REACH)
        ]

    def swapped(array):
        return lax.ppermute(array, "ctx", [(c, c ^ 1) for c in range(ctx_count)])

    def half(array, which):
        width = array.shape[-1] // 2
        return lax.dynamic_slice_in_dim(array, which * width, width, array.ndim - 1)

    def in_order(own, got, later_first, axis):
        own_first = (core == 1) if later_first else (core == 0)
        return jnp.stack(
            [jnp.where(own_first, own, got), jnp.where(own_first, got, own)], axis=axis
        )

    def sink_terms(sink_part):
        mine = jnp.sum(sink_part[:, :, 0].reshape(HEADS, 2, QUERY_PER_KV), axis=1).reshape(-1)
        mine = jnp.concatenate([mine, mine])
        return jnp.where(jnp.arange(HQ) // (HQ // 2) == core, mine, 0.0)

    def summed(terms, sent):
        total = terms[0].astype(jnp.float32)
        for other in sent:
            total = total + other.astype(jnp.float32)
        return total.astype(jnp.bfloat16)

    def halves(which):
        return jnp.stack([half(keys[:, 0], which), half(values[:, 0], which)], axis=1)

    piece = in_order(halves(core), swapped(halves(1 - core)), True, 2)
    pieces = [piece[relay] for relay in range(RELAY_COUNT)]
    pieces[0], pieces[1], mate = lax.optimization_barrier((pieces[0], pieces[1], 1 - core))
    mine_first = [pieces[first]] + shifted([pieces[first]], 1)
    got = swapped(
        jnp.stack([half(queries[:, 0], mate), half(output_gradient[:, 0], mate)])
    )
    mine_second = [pieces[second]] + shifted([pieces[second]], 1)
    attention, query_grad, out_send, *terms_first, sink_part = attend(
        first, doc_tiles, sink_logits, queries, output_gradient, got, mine_first, []
    )
    mine_second, sink_first = lax.optimization_barrier((mine_second, sink_part))
    sent_first = shifted(terms_first, -1)
    attention, query_grad, out_send, *terms_second, sink_part = attend(
        second,
        doc_tiles,
        sink_logits,
        queries,
        output_gradient,
        got,
        mine_second,
        [attention, query_grad, out_send],
    )
    sent_first, sink_first, sink_part, out_send, terms_second = lax.optimization_barrier(
        (sent_first, sink_first, sink_part, out_send, terms_second)
    )
    sent_second = shifted(terms_second, -1)
    out_got = swapped(out_send)
    out_got, sink_first = lax.optimization_barrier((out_got, sink_first))
    sink_grad = sink_terms(sink_part) + lax.ppermute(
        sink_terms(sink_first),
        "section",
        [(s, section_count - 1 - s) for s in range(section_count)],
    )
    for turn, distance in enumerate((8, 4, 2, 1)):
        if turn == 2:
            sent_second, sink_grad = lax.optimization_barrier((sent_second, sink_grad))
        sink_grad = sink_grad + lax.ppermute(
            sink_grad, "ctx", [(c, c ^ distance) for c in range(ctx_count)]
        )
    place = (0, 0, 0, mate * QUERY_PART)
    attention = lax.dynamic_update_slice(attention, out_got[:, :1], place)
    query_grad = lax.dynamic_update_slice(query_grad, out_got[:, 1:], place)
    first_sum = summed(terms_first, sent_first)
    sent_second, first_sum, attention, query_grad = lax.optimization_barrier(
        (sent_second, first_sum, attention, query_grad)
    )
    second_sum = summed(terms_second, sent_second)
    sums = jnp.stack([second_sum, first_sum])
    own = lax.dynamic_index_in_dim(sums, mate, 2, keepdims=False)
    got = swapped(lax.dynamic_index_in_dim(sums, core, 2, keepdims=False))
    grads = jnp.concatenate(
        [jnp.where(core == 0, own, got), jnp.where(core == 0, got, own)], axis=-1
    )
    return (attention, query_grad, grads[:, :1], grads[:, 1:], sink_grad[None])


def solution(mesh):
    placed = (
        P(None, "section", "ctx", None),
        P(None, "section", "ctx", None),
        P(None, "section", "ctx", None),
        P(None, "section", "ctx", None),
        P(None, "section", None),
        P(),
    )
    return jax.shard_map(
        shards,
        mesh=mesh,
        in_specs=placed,
        out_specs=(
            P(None, "section", "ctx", None),
            P(None, "section", "ctx", None),
            P(None, "section", "ctx", None),
            P(None, "section", "ctx", None),
            P("section", None),
        ),
        check_vma=False,
    )
```

```python
import functools
import math

import jax
import jax.numpy as jnp
from jax import lax
from jax.experimental import pallas as pl
from jax.experimental.pallas import tpu as pltpu
from jax.sharding import PartitionSpec as P

HEAD_WIDTH = 128
HQ = 32
KEY_HEADS = 4
QUERY_PER_KV = 8
TILE = 128
DOCS = 4
RELAY_COUNT = 2
LONGEST = 9
REACH = LONGEST // 2
ROWS = QUERY_PER_KV * TILE
SCALE = 1.0 / math.sqrt(HEAD_WIDTH)
LOG2E = 1.4426950408889634
HIDDEN = -1e30
VMEM_BYTES = 20 * 1024 * 1024
GROUP = 3
SLOTS = 2 * (REACH + 1)
HEADS = KEY_HEADS // 2
STEPS = 2 * HEADS
KEY_PART = HEADS * HEAD_WIDTH
WIDE = QUERY_PER_KV * HEAD_WIDTH
QUERY_PART = HEADS * WIDE


def dot(left, right, left_dim, right_dim):
    return lax.dot_general(
        left,
        right,
        (((left_dim,), (right_dim,)), ((), ())),
        preferred_element_type=jnp.float32,
    )


def attend_kernel(relay, refilled, doc_tiles, sink, q_own, g_own, got, *refs):
    pieces = refs[: REACH + 1]
    refs = refs[REACH + 1 + refilled :]
    o_ref, dq_ref, out_send = refs[:3]
    terms = refs[3 : REACH + 4]
    sink_part = refs[REACH + 4]
    q_in, g_in, o_out, dq_out, kv, grads, grads_low = refs[REACH + 5 : REACH + 12]
    g_turned, q_rows, g_rows, scores, shares, out_sum, dq_sum = refs[REACH + 12 : REACH + 19]
    q_sem, kv_sem, out_sem, grad_sem = refs[REACH + 19 :]
    step = pl.program_id(0)
    head = lax.div(step, 2)
    later = lax.rem(step, 2)
    ctx_pos = lax.axis_index("ctx")
    section_pos = lax.axis_index("section")
    core = lax.rem(ctx_pos, 2)
    layer = section_pos if relay == 0 else lax.axis_size("section") - 1 - section_pos
    position = ctx_pos - core + later
    end = start = jnp.int32(0)
    for document in range(DOCS):
        end = end + doc_tiles[relay, 0, document]
        start = jnp.where(end <= position, end, start)
    count = position - start + 1
    groups = lax.div(count + GROUP - 1, GROUP)
    offset = 1 - later

    def wide_cols(j):
        return pl.ds(pl.multiple_of(j * WIDE, WIDE), WIDE)

    def fetch_rows(i, own):
        pairs = ((q_own, q_in), (g_own, g_in))
        return [
            pltpu.make_async_copy(
                mine.at[relay, 0, :, wide_cols(HEADS * core + i // 2)]
                if own
                else got.at[k, relay, :, pl.ds((i // 2) * WIDE, WIDE)],
                to.at[i],
                q_sem.at[k, i],
            )
            for k, (mine, to) in enumerate(pairs)
        ]

    def fetch_keys(j, distance):
        return pltpu.make_async_copy(
            pieces[distance].at[:, :, :, pl.ds(j * HEAD_WIDTH, HEAD_WIDTH)],
            kv.at[j, :, pl.ds(2 * distance, 2)],
            kv_sem.at[j, distance],
        )

    def give_rows(i, own):
        return [
            pltpu.make_async_copy(
                source.at[i],
                target.at[relay, 0, :, wide_cols(HEADS * core + i // 2)]
                if own
                else out_send.at[relay, k, :, pl.ds((i // 2) * WIDE, WIDE)],
                out_sem.at[k, i],
            )
            for k, (source, target) in enumerate(((o_out, o_ref), (dq_out, dq_ref)))
        ]

    def give_grads(j, distance):
        return pltpu.make_async_copy(
            grads_low.at[j, :, pl.ds(2 * distance, 2)],
            terms[distance].at[:, :, :, pl.ds(j * HEAD_WIDTH, HEAD_WIDTH)],
            grad_sem.at[j, distance],
        )

    def start_all(copies):
        for copy in copies:
            copy.start()

    def wait_all(copies):
        for copy in copies:
            copy.wait()

    @pl.when(step == 0)
    def _():
        for i in range(STEPS):
            pl.when(core == i % 2)(lambda: start_all(fetch_rows(i, True)))
            pl.when(core != i % 2)(lambda: start_all(fetch_rows(i, False)))
            if i % 2 == 0:
                start_all(fetch_keys(i // 2, distance) for distance in range(REACH + 1))

    for i in range(STEPS):

        @pl.when(step == i)
        def _():
            wait_all(fetch_rows(i, False))
            if i % 2 == 0:
                wait_all(fetch_keys(i // 2, distance) for distance in range(REACH + 1))

    heads = [slice(i * HEAD_WIDTH, (i + 1) * HEAD_WIDTH) for i in range(QUERY_PER_KV)]
    for part in heads:
        q, g = q_in[step, :, part], g_in[step, :, part]
        q_rows[part, :] = q
        g_rows[part, :] = g
        g_turned[:, part] = g.T

    def tiles_of(which, group):
        rows = kv[head, which, pl.ds(offset + group * GROUP, GROUP)]
        return rows.reshape(GROUP * TILE, HEAD_WIDTH)

    def block(group):
        return pl.ds(pl.multiple_of(group * GROUP * TILE, GROUP * TILE), GROUP * TILE)

    def scores_of(group):
        score = dot(tiles_of(0, group), q_rows[...], 1, 1)
        rows = [score[:TILE]]
        for i in range(1, GROUP):
            bias = jnp.where(GROUP * group + i < count, 0.0, HIDDEN).astype(jnp.float32)
            rows.append(score[i * TILE : (i + 1) * TILE] + bias)
        return rows

    def keep_scores(group, rows, top):
        score = jnp.concatenate(rows, axis=0)
        scores[block(group), :] = score
        most = jnp.max(score.reshape(-1, 8, ROWS), axis=0)
        return most if top is None else jnp.maximum(top, most)

    row = lax.broadcasted_iota(jnp.int32, (TILE, TILE), 0)
    column = lax.broadcasted_iota(jnp.int32, (TILE, TILE), 1)
    seen = jnp.concatenate([row <= column] * QUERY_PER_KV, axis=1)
    rows = scores_of(0)
    top = keep_scores(0, [jnp.where(seen, rows[0], HIDDEN)] + rows[1:], None)
    top = lax.fori_loop(
        1, groups, lambda group, top: keep_scores(group, scores_of(group), top), top
    )
    logit = jnp.concatenate(
        [
            jnp.full(
                (1, TILE), sink[layer, (HEADS * core + head) * QUERY_PER_KV + i] * LOG2E, jnp.float32
            )
            for i in range(QUERY_PER_KV)
        ],
        axis=1,
    )
    top = jnp.maximum(jnp.max(top, axis=0, keepdims=True) * (SCALE * LOG2E), logit)

    out_sum[...] = jnp.zeros_like(out_sum)
    dq_sum[...] = jnp.zeros_like(dq_sum)
    ones = jnp.ones((16, GROUP * TILE), jnp.bfloat16)

    def share_step(group, carry):
        turned = jnp.concatenate([tiles_of(1, group).T, ones], axis=0)
        low = jnp.exp2(scores[block(group), :] * (SCALE * LOG2E) - top).astype(jnp.bfloat16)
        shares[block(group), :] = low
        out_sum[...] += dot(turned, low, 1, 0)
        return carry

    lax.fori_loop(0, groups, share_step, 0)
    sink_raised = jnp.exp2(logit - top)
    inverse = 1.0 / (out_sum[HEAD_WIDTH : HEAD_WIDTH + 1, :] + sink_raised)
    out = (out_sum[:HEAD_WIDTH, :] * inverse).astype(jnp.bfloat16)
    delta = jnp.sum(
        out.astype(jnp.float32) * g_turned[...].astype(jnp.float32), axis=0, keepdims=True
    )
    sink_rows = sink_raised * inverse * delta
    for i, part in enumerate(heads):
        o_out[step, :, part] = out[:, part].T
        sink_part[0, i : i + 1, :] = jnp.broadcast_to(
            -jnp.sum(sink_rows[:, part], axis=1, keepdims=True), (1, HEAD_WIDTH)
        )

    @pl.when(later == 0)
    def _():
        grads[...] = jnp.zeros_like(grads)

    def add_grads(which, group, term):
        rows = pl.ds(offset + group * GROUP, GROUP)
        grads[which, rows] += term.reshape(GROUP, TILE, HEAD_WIDTH)

    def grad_step(group, carry):
        share = shares[block(group), :].astype(jnp.float32) * inverse
        share_grad = dot(tiles_of(1, group), g_turned[...], 1, 0)
        score_grad = (share * (share_grad - delta)).astype(jnp.bfloat16)
        dq_sum[...] += dot(tiles_of(0, group).T, score_grad, 1, 0)
        add_grads(0, group, dot(score_grad, q_rows[...], 1, 0))
        add_grads(1, group, dot(share.astype(jnp.bfloat16), g_rows[...], 1, 0))
        return carry

    lax.fori_loop(0, groups, grad_step, 0)
    for part in heads:
        dq_out[step, :, part] = (dq_sum[:, part] * SCALE).astype(jnp.bfloat16).T

    @pl.when(later == 1)
    def _():
        grads_low[head, 0] = (grads[0] * SCALE).astype(jnp.bfloat16)
        grads_low[head, 1] = grads[1].astype(jnp.bfloat16)

    for i in range(STEPS):

        @pl.when(step == i)
        def _():
            pl.when(core == i % 2)(lambda: start_all(give_rows(i, True)))
            pl.when(core != i % 2)(lambda: start_all(give_rows(i, False)))
            if i % 2 == 1:
                start_all(give_grads(i // 2, distance) for distance in range(REACH + 1))

    @pl.when(step == STEPS - 1)
    def _():
        for i in range(STEPS):
            wait_all(give_rows(i, False))
            if i % 2 == 1:
                wait_all(give_grads(i // 2, distance) for distance in range(REACH + 1))


def attend(relay, doc_tiles, sink_logits, queries, output_gradient, got, pieces, filled):
    smem = pl.BlockSpec(memory_space=pltpu.SMEM)
    whole = pl.BlockSpec(memory_space=pl.ANY)
    low = jnp.bfloat16
    inputs = [queries, output_gradient, got, *pieces, *filled]
    first = 2 + len(inputs) - len(filled)
    rows = pltpu.VMEM((STEPS, TILE, WIDE), low)
    return pl.pallas_call(
        functools.partial(attend_kernel, relay, len(filled)),
        grid=(STEPS,),
        in_specs=[smem, smem] + [whole] * len(inputs),
        out_specs=[whole] * (REACH + 4)
        + [pl.BlockSpec((1, QUERY_PER_KV, HEAD_WIDTH), lambda i: (i, 0, 0))],
        out_shape=[
            jax.ShapeDtypeStruct(queries.shape, low),
            jax.ShapeDtypeStruct(queries.shape, low),
            jax.ShapeDtypeStruct((RELAY_COUNT, 2, TILE, QUERY_PART), low),
        ]
        + [jax.ShapeDtypeStruct((2, 2, TILE, KEY_PART), low)] * (REACH + 1)
        + [jax.ShapeDtypeStruct((STEPS, QUERY_PER_KV, HEAD_WIDTH), jnp.float32)],
        scratch_shapes=[
            rows,
            rows,
            rows,
            rows,
            pltpu.VMEM((HEADS, 2, SLOTS, TILE, HEAD_WIDTH), low),
            pltpu.VMEM((2, SLOTS, TILE, HEAD_WIDTH), jnp.float32),
            pltpu.VMEM((HEADS, 2, SLOTS, TILE, HEAD_WIDTH), low),
            pltpu.VMEM((HEAD_WIDTH, ROWS), low),
            pltpu.VMEM((ROWS, HEAD_WIDTH), low),
            pltpu.VMEM((ROWS, HEAD_WIDTH), low),
            pltpu.VMEM((LONGEST * TILE, ROWS), jnp.float32),
            pltpu.VMEM((LONGEST * TILE, ROWS), low),
            pltpu.VMEM((HEAD_WIDTH + 16, ROWS), jnp.float32),
            pltpu.VMEM((HEAD_WIDTH, ROWS), jnp.float32),
            pltpu.SemaphoreType.DMA((2, STEPS)),
            pltpu.SemaphoreType.DMA((HEADS, REACH + 1)),
            pltpu.SemaphoreType.DMA((2, STEPS)),
            pltpu.SemaphoreType.DMA((HEADS, REACH + 1)),
        ],
        input_output_aliases={first + i: i for i in range(len(filled))},
        compiler_params=pltpu.CompilerParams(vmem_limit_bytes=VMEM_BYTES),
        cost_estimate=pl.CostEstimate(
            flops=12 * LONGEST * HQ * TILE * TILE * HEAD_WIDTH * 4,
            bytes_accessed=9 << 20,
            transcendentals=LONGEST * HQ * TILE * TILE,
        ),
        name=f"attend_{relay}",
    )(doc_tiles, sink_logits, *inputs)


def shards(queries, keys, values, output_gradient, doc_tiles, sink_logits):
    ctx_count = lax.axis_size("ctx")
    ctx_pos = lax.axis_index("ctx")
    section_pos = lax.axis_index("section")
    section_count = lax.axis_size("section")
    core = lax.rem(ctx_pos, 2)
    first, second = 1, 0

    def shifted(pieces, amount):
        route = [
            (c, c + amount * 2 * (distance + 1))
            for distance in range(REACH)
            for c in range(ctx_count)
        ]
        routes = [route[d * ctx_count : (d + 1) * ctx_count] for d in range(REACH)]
        return [
            lax.ppermute(
                pieces[d + 1] if len(pieces) > 1 else pieces[0],
                "ctx",
                [(a, b) for a, b in routes[d] if 0 <= b < ctx_count],
            )
            for d in range(REACH)
        ]

    def swapped(array):
        return lax.ppermute(array, "ctx", [(c, c ^ 1) for c in range(ctx_count)])

    def half(array, which):
        width = array.shape[-1] // 2
        return lax.dynamic_slice_in_dim(array, which * width, width, array.ndim - 1)

    def in_order(own, got, later_first, axis):
        own_first = (core == 1) if later_first else (core == 0)
        return jnp.stack(
            [jnp.where(own_first, own, got), jnp.where(own_first, got, own)], axis=axis
        )

    def sink_terms(sink_part):
        mine = jnp.sum(sink_part[:, :, 0].reshape(HEADS, 2, QUERY_PER_KV), axis=1).reshape(-1)
        mine = jnp.concatenate([mine, mine])
        return jnp.where(jnp.arange(HQ) // (HQ // 2) == core, mine, 0.0)

    def summed(terms, sent):
        total = terms[0].astype(jnp.float32)
        for other in sent:
            total = total + other.astype(jnp.float32)
        return total.astype(jnp.bfloat16)

    def halves(which):
        return jnp.stack([half(keys[:, 0], which), half(values[:, 0], which)], axis=1)

    piece = in_order(halves(core), swapped(halves(1 - core)), True, 2)
    pieces = [piece[relay] for relay in range(RELAY_COUNT)]
    pieces[0], pieces[1], mate = lax.optimization_barrier((pieces[0], pieces[1], 1 - core))
    mine_first = [pieces[first]] + shifted([pieces[first]], 1)
    got = swapped(
        jnp.stack([half(queries[:, 0], mate), half(output_gradient[:, 0], mate)])
    )
    mine_second = [pieces[second]] + shifted([pieces[second]], 1)
    attention, query_grad, out_send, *terms_first, sink_part = attend(
        first, doc_tiles, sink_logits, queries, output_gradient, got, mine_first, []
    )
    mine_second, sink_first = lax.optimization_barrier((mine_second, sink_part))
    sent_first = shifted(terms_first, -1)
    attention, query_grad, out_send, *terms_second, sink_part = attend(
        second,
        doc_tiles,
        sink_logits,
        queries,
        output_gradient,
        got,
        mine_second,
        [attention, query_grad, out_send],
    )
    sent_first, sink_first, sink_part, out_send, terms_second = lax.optimization_barrier(
        (sent_first, sink_first, sink_part, out_send, terms_second)
    )
    sent_second = shifted(terms_second, -1)
    out_got = swapped(out_send)
    out_got, sink_first = lax.optimization_barrier((out_got, sink_first))
    sink_grad = sink_terms(sink_part) + lax.ppermute(
        sink_terms(sink_first),
        "section",
        [(s, section_count - 1 - s) for s in range(section_count)],
    )
    distance = 1
    while distance < ctx_count:
        sink_grad = sink_grad + lax.ppermute(
            sink_grad, "ctx", [(c, c ^ distance) for c in range(ctx_count)]
        )
        distance *= 2
    place = (0, 0, 0, mate * QUERY_PART)
    attention = lax.dynamic_update_slice(attention, out_got[:, :1], place)
    query_grad = lax.dynamic_update_slice(query_grad, out_got[:, 1:], place)
    first_sum = summed(terms_first, sent_first)
    sent_second, sink_grad, first_sum, attention, query_grad = lax.optimization_barrier(
        (sent_second, sink_grad, first_sum, attention, query_grad)
    )
    second_sum = summed(terms_second, sent_second)
    sums = jnp.stack([second_sum, first_sum])
    own = lax.dynamic_index_in_dim(sums, mate, 2, keepdims=False)
    got = swapped(lax.dynamic_index_in_dim(sums, core, 2, keepdims=False))
    grads = jnp.concatenate(
        [jnp.where(core == 0, own, got), jnp.where(core == 0, got, own)], axis=-1
    )
    return (attention, query_grad, grads[:, :1], grads[:, 1:], sink_grad[None])


def solution(mesh):
    placed = (
        P(None, "section", "ctx", None),
        P(None, "section", "ctx", None),
        P(None, "section", "ctx", None),
        P(None, "section", "ctx", None),
        P(None, "section", None),
        P(),
    )
    return jax.shard_map(
        shards,
        mesh=mesh,
        in_specs=placed,
        out_specs=(
            P(None, "section", "ctx", None),
            P(None, "section", "ctx", None),
            P(None, "section", "ctx", None),
            P(None, "section", "ctx", None),
            P("section", None),
        ),
        check_vma=False,
    )
```
